128 devices in a mesh: row: 8 (over z, core), col: 16 (over x, y).
Axes of the slice: x: 4, y: 4, z: 4, core: 2. Of those that a mesh axis runs over, the one named last changes fastest.
Arguments:
- stored: float32 [16384, 16384], P('row', 'col'), may hold values from -2 to 72, as said below
Outputs:
- trailing: float32 [16384, 16384], P('row', 'col')
- factor: float32 [16384, 256], P('row')
The draws below stay inside these ranges and needn't reach their ends.
Inputs may be any that keep to these rules, and one draw needn't show every extreme that they name: stored is the block-cyclic storage of a symmetric positive definite matrix whose two leading block columns are well conditioned.
All inputs are finite; a program needn't handle non-finite values.
Results may differ from the reference program's by a relative error of at most 0.00012.
Values sent between devices are 32-bit elements; how exact they have to be, the bound alone decides.
No kernel may reach another device: no remote copies, remote signals or barrier semaphores. Data moves between devices by JAX's collectives and lax.ppermute only.
A program may use at most 128 MiB of HBM per device.

```python
import math
import jax
import jax.numpy as jnp
from jax import lax

BLOCK = 128
PANELS = 2
M = 16384
N_ROW = 8
N_COL = 16


def storage_rows(matrix, parts):
    count = matrix.shape[0]
    shaped = matrix.reshape(count // (parts * BLOCK), parts, BLOCK, matrix.shape[1])
    return shaped.transpose(1, 0, 2, 3).reshape(matrix.shape)


def draw_stored(key, part):
    key = jax.random.fold_in(key, 1)
    first_key, second_key = jax.random.split(key)
    noise = jax.random.normal(first_key, (M, M), jnp.float32)
    spread = jax.random.uniform(second_key, (M,), jnp.float32, 1.0, 1.25)
    symmetric = (noise + noise.T) * jnp.float32(math.sqrt(0.5))
    index = jnp.arange(M)
    head = index < 2 * BLOCK
    both_head = head[:, None] & head[None, :]
    one_head = head[:, None] != head[None, :]
    scale = jnp.where(both_head, 0.05, jnp.where(one_head, 1.0 / 16.0, 1.0 / math.sqrt(M)))
    diag_values = jnp.where(head, 4.0, M / 512.0 + 4.0) * spread
    equal = index[:, None] == index[None, :]
    matrix = jnp.where(equal, diag_values[:, None], symmetric * scale)
    matrix = jnp.clip(matrix, -2.0, 2.0 * (M // 512 + 4))
    return storage_rows(storage_rows(matrix, N_ROW).T, N_COL).T.astype(jnp.float32)


def setup_inputs(seed: int = 0) -> dict:
    key_list = jax.random.split(jax.random.key(seed), 2)
    return {
        "stored": draw_stored(jax.random.fold_in(key_list[1], 71), 0),
    }


def rows_to_natural(matrix, parts):
    count = matrix.shape[0]
    shaped = matrix.reshape(parts, count // (parts * BLOCK), BLOCK, matrix.shape[1])
    return shaped.transpose(1, 0, 2, 3).reshape(matrix.shape)

def rows_to_storage(matrix, parts):
    count = matrix.shape[0]
    shaped = matrix.reshape(count // (parts * BLOCK), parts, BLOCK, matrix.shape[1])
    return shaped.transpose(1, 0, 2, 3).reshape(matrix.shape)

def reference(stored):
    natural = rows_to_natural(rows_to_natural(stored, N_ROW).T, N_COL).T
    block_index = jnp.arange(M) // BLOCK
    panels = []
    for panel_index in range(PANELS):
        column = natural[:, panel_index * BLOCK:(panel_index + 1) * BLOCK]
        diag_block = column[panel_index * BLOCK:(panel_index + 1) * BLOCK]
        lower = jnp.linalg.cholesky(diag_block)
        solved = jax.scipy.linalg.solve_triangular(lower, column.T, lower=True).T
        solved = jnp.where((block_index < panel_index)[:, None], jnp.float32(0.0), solved)
        solved = solved.at[panel_index * BLOCK:(panel_index + 1) * BLOCK].set(lower)
        panels.append(solved)
        natural = natural - jnp.dot(solved.astype(jnp.float32), solved.T.astype(jnp.float32), precision=lax.Precision.HIGHEST, preferred_element_type=jnp.float32)
    trailing = rows_to_storage(rows_to_storage(natural, N_ROW).T, N_COL).T
    factor = rows_to_storage(jnp.concatenate(panels, axis=1), N_ROW)
    return (trailing, factor)
```

```python
import functools

import jax
import jax.numpy as jnp
from jax import lax
from jax.experimental import pallas as pl
from jax.experimental.pallas import tpu as pltpu
from jax.sharding import PartitionSpec as P

BLOCK = 128
WIDE = 2 * BLOCK
GROUP = 4
TILE = 256
F32 = jnp.float32
BF16 = jnp.bfloat16
AXES = ("row", "col")
NT = (((1,), (1,)), ((), ()))
NN = (((1,), (0,)), ((), ()))


def exact(left, right, dims):
    return lax.dot_general(
        left, right, dims, precision=lax.Precision.HIGHEST, preferred_element_type=F32
    )


def eliminate(matrix):
    lane = lax.broadcasted_iota(jnp.int32, (8, BLOCK), 1)
    sub = lax.broadcasted_iota(jnp.int32, (8, BLOCK), 0)
    rows = [matrix[8 * i : 8 * i + 8, :] for i in range(BLOCK // 8)]
    for first in range(0, BLOCK, GROUP):
        at = first // 8
        cols = {}
        for j in range(GROUP):
            for i in range(at, BLOCK // 8):
                cols[j, i] = jnp.broadcast_to(rows[i][:, first + j : first + j + 1], (8, BLOCK))
        for j in range(GROUP):
            k = first + j
            s = k % 8
            here = lane == k
            pivot = 1.0 / cols[j, at][s : s + 1, :]
            row = jnp.where(here[:1], 1.0, rows[at][s : s + 1, :])
            heads = {m: cols[m, at][s : s + 1, :] for m in range(j + 1, GROUP)}
            for i in range(at, BLOCK // 8):
                factor = cols[j, i] * pivot
                if i == at:
                    factor = jnp.where(sub > s, factor, 0.0)
                    rows[i] = jnp.where(here & (sub > s), 0.0, rows[i]) - factor * row
                else:
                    rows[i] = jnp.where(here, 0.0, rows[i]) - factor * row
                for m in range(j + 1, GROUP):
                    cols[m, i] = cols[m, i] - factor * heads[m]
    return jnp.concatenate(rows, axis=0)


def factor_block(matrix):
    done = eliminate(matrix)
    r = lax.broadcasted_iota(jnp.int32, (BLOCK, BLOCK), 0)
    c = lax.broadcasted_iota(jnp.int32, (BLOCK, BLOCK), 1)
    pivots = jnp.sum(jnp.where(r == c, done, 0.0), axis=1, keepdims=True)
    scale = lax.rsqrt(pivots)
    scale = scale * (1.5 - 0.5 * pivots * scale * scale)
    upper = jnp.where(r <= c, done, 0.0) * scale
    inverse = jnp.where(r > c, done, jnp.where(r == c, 1.0, 0.0)) * scale
    return upper.T, inverse


def head_kernel(diag_ref, lower_ref, inverse_ref):
    zero = jnp.zeros((BLOCK, BLOCK), F32)
    l00, i00 = factor_block(diag_ref[0])
    l10 = exact(diag_ref[1], i00, NT)
    l11, i11 = factor_block(diag_ref[2] - exact(l10, l10, NT))
    i10 = -exact(i11, exact(l10, i00, NN), NN)
    lower_ref[0, :, :BLOCK] = l00
    lower_ref[0, :, BLOCK:] = zero
    lower_ref[1, :, :BLOCK] = l10
    lower_ref[1, :, BLOCK:] = l11
    inverse_ref[:BLOCK, :BLOCK] = i00
    inverse_ref[:BLOCK, BLOCK:] = zero
    inverse_ref[BLOCK:, :BLOCK] = i10
    inverse_ref[BLOCK:, BLOCK:] = i11


def head(diag):
    return pl.pallas_call(
        head_kernel,
        out_shape=(
            jax.ShapeDtypeStruct((2, BLOCK, WIDE), F32),
            jax.ShapeDtypeStruct((WIDE, WIDE), F32),
        ),
        cost_estimate=pl.CostEstimate(flops=10**8, bytes_accessed=10**6, transcendentals=0),
        name="head",
    )(diag)


def split(x):
    high = x.astype(BF16)
    return high, (x - high.astype(F32)).astype(BF16)


def update_kernel(where_ref, lower_ref, inverse_ref, row_ref, col_ref, a_ref, out_ref, factor_ref, right_ref):
    my_row = where_ref[0]
    my_col = where_ref[1]

    @pl.when(pl.program_id(0) == 0)
    def _():
        def put(columns, start, width):
            high, low = split(columns)
            right_ref[0:WIDE, start : start + width] = high
            right_ref[WIDE : 2 * WIDE, start : start + width] = low
            right_ref[2 * WIDE : 3 * WIDE, start : start + width] = high

        for start in range(0, col_ref.shape[1], WIDE):
            put(exact(inverse_ref[...], col_ref[:, start : start + WIDE], NN), start, WIDE)

        @pl.when(my_col < 2)
        def _():
            put(lower_ref[my_col].T, 0, BLOCK)

    factor_ref[...] = exact(row_ref[...], inverse_ref[...], NT)

    @pl.when((pl.program_id(0) == 0) & (my_row < 2))
    def _():
        factor_ref[0:BLOCK, :] = lower_ref[my_row]

    high, low = split(factor_ref[...])
    left = jnp.concatenate([high, high, low], axis=1)
    out_ref[...] = a_ref[...] - lax.dot_general(left, right_ref[...], NN, preferred_element_type=F32)


def update(where, lower, inverse, row_part, col_part, stored):
    rows, cols = stored.shape
    grid_spec = pltpu.PrefetchScalarGridSpec(
        num_scalar_prefetch=1,
        grid=(rows // TILE,),
        in_specs=[
            pl.BlockSpec((2, BLOCK, WIDE), lambda i, w: (0, 0, 0)),
            pl.BlockSpec((WIDE, WIDE), lambda i, w: (0, 0)),
            pl.BlockSpec((TILE, WIDE), lambda i, w: (i, 0)),
            pl.BlockSpec((WIDE, cols), lambda i, w: (0, 0)),
            pl.BlockSpec((TILE, cols), lambda i, w: (i, 0)),
        ],
        out_specs=[
            pl.BlockSpec((TILE, cols), lambda i, w: (i, 0)),
            pl.BlockSpec((TILE, WIDE), lambda i, w: (i, 0)),
        ],
        scratch_shapes=[pltpu.VMEM((3 * WIDE, cols), BF16)],
    )
    return pl.pallas_call(
        update_kernel,
        grid_spec=grid_spec,
        out_shape=(
            jax.ShapeDtypeStruct((rows, cols), F32),
            jax.ShapeDtypeStruct((rows, WIDE), F32),
        ),
        compiler_params=pltpu.CompilerParams(vmem_limit_bytes=40 * 2**20),
        name="update",
    )(where, lower, inverse, row_part, col_part, stored)


def on_device(stored, n_row, n_col):
    my_row = lax.axis_index("row")
    my_col = lax.axis_index("col")
    core = my_row % 2
    depth = my_row // 2

    def at(r, c):
        return r * n_col + c

    def send(x, pairs):
        return lax.ppermute(x, AXES, pairs)

    corner = stored[:BLOCK, :BLOCK]
    other = send(corner, [(at(r, c), at(1 - r, c)) for r in (0, 1) for c in (0, 1)])
    half = jnp.where(core == 0, jnp.stack([corner, other]), jnp.stack([other, corner]))
    other = send(half, [(at(r, c), at(r, 1 - c)) for r in (0, 1) for c in (0, 1)])
    first, second = jnp.where(my_col == 0, half, other), jnp.where(my_col == 0, other, half)
    diag = jnp.stack([first[0], first[1], second[1]])
    got = [
        send(diag, [(at(r, c), at(r, c + 4 * d)) for r in (0, 1) for c in (0, 1)])
        for d in (1, 3, 2)
    ]
    diag = jnp.where(my_col < 2, diag, got[0] + got[1] + got[2])
    have = [(r, 4 * x + y) for r in (0, 1) for x in range(4) for y in (0, 1)]
    got = [send(diag, [(at(r, c), at(r + 2 * d, c)) for r, c in have]) for d in (1, 3, 2)]
    diag = jnp.where(my_row < 2, diag, got[0] + got[1] + got[2])
    have = [(r, 4 * x + y) for r in range(n_row) for x in range(4) for y in (0, 1)]
    got = send(diag, [(at(r, c), at(r, c - c % 4 + 3 - c % 4)) for r, c in have])
    diag = jnp.where(my_col % 4 < 2, diag, got)

    strip = stored[:BLOCK].reshape(BLOCK, n_row // 2, 2, BLOCK)
    keep = lax.dynamic_index_in_dim(strip, core, 2, False).transpose(1, 0, 2)
    give = lax.dynamic_index_in_dim(strip, 1 - core, 2, False).transpose(1, 0, 2)
    other = send(give, [(at(r, c), at(1 - r, c)) for r in (0, 1) for c in range(n_col)])
    both = jnp.where(core == 0, jnp.stack([keep, other], 1), jnp.stack([other, keep], 1))
    got = [
        send(both[d], [(at(r, c), at(r + 2 * d, c)) for r in (0, 1) for c in range(n_col)])
        for d in (1, 3, 2)
    ]
    block = jnp.where(depth == 0, both[0], got[0] + got[1] + got[2]).reshape(WIDE, BLOCK)
    col_part = lax.all_gather(block, "row", axis=0, tiled=False)
    col_part = col_part.transpose(1, 0, 2).reshape(WIDE, n_row * BLOCK)

    turned = send(
        block,
        [(at(r, c), at(c % n_row, 2 * r + c // n_row)) for r in range(n_row) for c in range(n_col)],
    )
    row_part = lax.all_gather(turned.T, "col", axis=0, tiled=True)

    lower, inverse = head(diag)
    where = jnp.stack([my_row, my_col]).astype(jnp.int32)
    trailing, factor = update(where, lower, inverse, row_part, col_part, stored)
    return trailing, factor


def solution(mesh):
    body = functools.partial(on_device, n_row=mesh.shape["row"], n_col=mesh.shape["col"])
    return jax.shard_map(
        body,
        mesh=mesh,
        in_specs=(P("row", "col"),),
        out_specs=(P("row", "col"), P("row", None)),
        check_vma=False,
    )
```

```python
import functools

import jax
import jax.numpy as jnp
from jax import lax
from jax.experimental import pallas as pl
from jax.experimental.pallas import tpu as pltpu
from jax.sharding import PartitionSpec as P

BLOCK = 128
WIDE = 2 * BLOCK
GROUP = 8
SHIFTS = (0, 1, 3, 2)
F32 = jnp.float32
BF16 = jnp.bfloat16
AXES = ("row", "col")
NT = (((1,), (1,)), ((), ()))
NN = (((1,), (0,)), ((), ()))


def exact(left, right, dims):
    return lax.dot_general(
        left, right, dims, precision=lax.Precision.HIGHEST, preferred_element_type=F32
    )


def eliminate(matrix):
    lane = lax.broadcasted_iota(jnp.int32, (8, BLOCK), 1)
    sub = lax.broadcasted_iota(jnp.int32, (8, BLOCK), 0)
    rows = [matrix[8 * i : 8 * i + 8, :] for i in range(BLOCK // 8)]
    for first in range(0, BLOCK, GROUP):
        at = first // 8
        cols = {}
        for j in range(GROUP):
            for i in range(at, BLOCK // 8):
                cols[j, i] = jnp.broadcast_to(rows[i][:, first + j : first + j + 1], (8, BLOCK))
        for j in range(GROUP):
            k = first + j
            s = k % 8
            here = lane == k
            pivot = 1.0 / cols[j, at][s : s + 1, :]
            row = jnp.where(here[:1], 1.0, rows[at][s : s + 1, :])
            heads = {m: cols[m, at][s : s + 1, :] for m in range(j + 1, GROUP)}
            for i in range(at, BLOCK // 8):
                factor = cols[j, i] * pivot
                if i == at:
                    factor = jnp.where(sub > s, factor, 0.0)
                    rows[i] = jnp.where(here & (sub > s), 0.0, rows[i]) - factor * row
                else:
                    rows[i] = jnp.where(here, 0.0, rows[i]) - factor * row
                for m in range(j + 1, GROUP):
                    cols[m, i] = cols[m, i] - factor * heads[m]
    return jnp.concatenate(rows, axis=0)


def factor_block(matrix):
    done = eliminate(matrix)
    r = lax.broadcasted_iota(jnp.int32, (BLOCK, BLOCK), 0)
    c = lax.broadcasted_iota(jnp.int32, (BLOCK, BLOCK), 1)
    pivots = jnp.sum(jnp.where(r == c, done, 0.0), axis=1, keepdims=True)
    scale = lax.rsqrt(pivots)
    scale = scale * (1.5 - 0.5 * pivots * scale * scale)
    upper = jnp.where(r <= c, done, 0.0) * scale
    inverse = jnp.where(r > c, done, jnp.where(r == c, 1.0, 0.0)) * scale
    return upper.T, inverse


def head_kernel(mine_ref, other_ref, lower_ref, inverse_ref):
    first = lax.axis_index("row") % 2 == 0
    zero = jnp.zeros((BLOCK, BLOCK), F32)
    l00, i00 = factor_block(jnp.where(first, mine_ref[0], other_ref[0]))
    l10 = exact(jnp.where(first, other_ref[0], mine_ref[0]), i00, NT)
    rest = jnp.where(first, other_ref[1], mine_ref[1]) - exact(l10, l10, NT)
    l11, i11 = factor_block(rest)
    i10 = -exact(i11, exact(l10, i00, NN), NN)
    lower_ref[0, :, :BLOCK] = l00
    lower_ref[0, :, BLOCK:] = zero
    lower_ref[1, :, :BLOCK] = l10
    lower_ref[1, :, BLOCK:] = l11
    inverse_ref[:BLOCK, :BLOCK] = i00
    inverse_ref[:BLOCK, BLOCK:] = zero
    inverse_ref[BLOCK:, :BLOCK] = i10
    inverse_ref[BLOCK:, BLOCK:] = i11


def head(mine, other):
    return pl.pallas_call(
        head_kernel,
        out_shape=(
            jax.ShapeDtypeStruct((2, BLOCK, WIDE), F32),
            jax.ShapeDtypeStruct((WIDE, WIDE), F32),
        ),
        cost_estimate=pl.CostEstimate(flops=10**8, bytes_accessed=10**6, transcendentals=0),
        name="head",
    )(mine, other)


def turn_kernel(in_ref, out_ref):
    for p in range(2):
        span = slice(p * BLOCK, (p + 1) * BLOCK)
        out_ref[:, span] = in_ref[span, :].T


def turn(block):
    return pl.pallas_call(
        turn_kernel, out_shape=jax.ShapeDtypeStruct((BLOCK, WIDE), F32), name="turn"
    )(block)


def split(x):
    high = x.astype(BF16)
    return high, (x - high.astype(F32)).astype(BF16)


def update_kernel(
    lower_ref, inverse_ref, row0_ref, row1_ref, row2_ref, row3_ref, tall_ref, beside_ref, a_ref, out_ref, factor_ref,
    a_buf, row_buf, factor_buf, col_buf, right_ref, a_sem, row_sem, col_sem, out_sem, factor_sem,
):
    my_row = lax.axis_index("row")
    my_col = lax.axis_index("col")
    x, y = my_col // 4, my_col % 4
    even = my_row % 2 == 0
    count, _, cols = a_ref.shape
    blocks = cols // BLOCK

    place = []
    for far in SHIFTS:
        for near in SHIFTS:
            dx = jnp.where(even, far, near)
            dy = jnp.where(even, near, far)
            place.append((x - dx + 4) % 4 * 4 + (y - dy + 4) % 4)

    def start(src, dst, sem):
        copy = pltpu.make_async_copy(src, dst, sem)
        copy.start()
        return copy

    col_in = []
    for b, d in enumerate(SHIFTS):
        depth = (my_row // 2 - d + 4) % 4 * 2
        col_in.append(start(tall_ref.at[b], col_buf.at[depth + my_row % 2], col_sem.at[b]))
        col_in.append(start(beside_ref.at[b], col_buf.at[depth + 1 - my_row % 2], col_sem.at[4 + b]))
    row_in = [
        start(ref, row_buf.at[a], row_sem.at[a])
        for a, ref in enumerate((row0_ref, row1_ref, row2_ref, row3_ref))
    ]
    a_in = [start(a_ref.at[place[t]], a_buf.at[t], a_sem.at[t]) for t in range(count)]

    high, low = split(inverse_ref[...])
    by_left = jnp.concatenate([high, high, low], axis=1)
    by_right = jnp.concatenate([high, low, high], axis=1)
    for copy in col_in:
        copy.wait()
    for b in range(0, blocks, 2):
        span = slice(b * BLOCK, (b + 2) * BLOCK)
        high, low = split(jnp.concatenate([col_buf[b], col_buf[b + 1]], axis=1))
        stack = jnp.concatenate([high, low, high], axis=0)
        part = lax.dot_general(by_left, stack, NN, preferred_element_type=F32)
        if b == 0:
            known = jnp.concatenate([lower_ref[jnp.minimum(my_col, 1)].T, part[:, BLOCK:]], axis=1)
            part = jnp.where(my_col < 2, known, part)
        high, low = split(part)
        right_ref[0:WIDE, span] = high
        right_ref[WIDE : 2 * WIDE, span] = low
        right_ref[2 * WIDE : 3 * WIDE, span] = high

    out = []
    for a in range(4):
        row_in[a].wait()
        high, low = split(row_buf[a].reshape(4 * BLOCK, WIDE))
        left = jnp.concatenate([high, high, low], axis=1)
        part = lax.dot_general(left, by_right, NT, preferred_element_type=F32)
        factor_buf[a] = part.reshape(4, BLOCK, WIDE)
        for s in range(4):
            t = 4 * a + s

            @pl.when((my_row < 2) & (place[t] == 0))
            def _():
                factor_buf[a, s] = lower_ref[jnp.minimum(my_row, 1)]

        for s in range(4):
            t = 4 * a + s
            out.append(start(factor_buf.at[a, s], factor_ref.at[place[t]], factor_sem.at[t]))
        high, low = split(factor_buf[a].reshape(4 * BLOCK, WIDE))
        left = jnp.concatenate([high, high, low], axis=1)
        for s in range(4):
            a_in[4 * a + s].wait()
        mine = slice(4 * a, 4 * a + 4)
        for n in range(0, cols, WIDE):
            span = slice(n, n + WIDE)
            part = lax.dot_general(left, right_ref[:, span], NN, preferred_element_type=F32)
            a_buf[mine, :, span] = a_buf[mine, :, span] - part.reshape(4, BLOCK, WIDE)
        for s in range(4):
            t = 4 * a + s
            out.append(start(a_buf.at[t], out_ref.at[place[t]], out_sem.at[t]))
    for copy in out:
        copy.wait()


def update(lower, inverse, row_parts, col_parts, stored):
    rows, cols = stored.shape
    count = rows // BLOCK
    here = pl.BlockSpec(memory_space=pltpu.VMEM)
    there = pl.BlockSpec(memory_space=pl.ANY)
    trailing, factor = pl.pallas_call(
        update_kernel,
        in_specs=[here] * 2 + [there] * 7,
        out_specs=[there] * 2,
        out_shape=(
            jax.ShapeDtypeStruct((count, BLOCK, cols), F32),
            jax.ShapeDtypeStruct((count, BLOCK, WIDE), F32),
        ),
        scratch_shapes=[
            pltpu.VMEM((count, BLOCK, cols), F32),
            pltpu.VMEM((4, 4, BLOCK, WIDE), F32),
            pltpu.VMEM((4, 4, BLOCK, WIDE), F32),
            pltpu.VMEM((cols // BLOCK, WIDE, BLOCK), F32),
            pltpu.VMEM((3 * WIDE, cols), BF16),
            pltpu.SemaphoreType.DMA((count,)),
            pltpu.SemaphoreType.DMA((4,)),
            pltpu.SemaphoreType.DMA((cols // BLOCK,)),
            pltpu.SemaphoreType.DMA((count,)),
            pltpu.SemaphoreType.DMA((count,)),
        ],
        compiler_params=pltpu.CompilerParams(vmem_limit_bytes=56 * 2**20),
        name="update",
    )(lower, inverse, *row_parts, *col_parts, stored.reshape(count, BLOCK, cols))
    return trailing.reshape(rows, cols), factor.reshape(rows, WIDE)


def on_device(stored, n_row, n_col):
    my_row = lax.axis_index("row")
    my_col = lax.axis_index("col")
    core = my_row % 2
    depth = my_row // 2

    def at(r, c):
        return r * n_col + c

    def send(x, pairs):
        return lax.ppermute(x, AXES, pairs)

    def near(phase, d):
        pairs = []
        for r in range(n_row):
            for c in range(n_col):
                x, y = divmod(c, 4)
                if (r % 2 == 0) == (phase == 1):
                    pairs.append((at(r, c), at(r, x * 4 + (y + d) % 4)))
                else:
                    pairs.append((at(r, c), at(r, (x + d) % 4 * 4 + y)))
        return pairs

    every_row, every_col = range(n_row), range(n_col)

    corner = stored[:BLOCK, :BLOCK]
    got = [send(corner, [(at(r, c), at(r + 2 * d, c)) for r in (0, 1) for c in (0, 1)]) for d in SHIFTS[1:]]
    strip = stored[:BLOCK].reshape(BLOCK, n_row // 2, 2, BLOCK)
    keep = lax.dynamic_index_in_dim(strip, core, 2, False).transpose(1, 0, 2)
    give = lax.dynamic_index_in_dim(strip, 1 - core, 2, False).transpose(1, 0, 2)
    other = send(give, [(at(r, c), at(1 - r, c)) for r in (0, 1) for c in every_col])
    both = jnp.where(core == 0, jnp.stack([keep, other], 1), jnp.stack([other, keep], 1))
    corner = jnp.where(depth == 0, corner, got[0] + got[1] + got[2])
    corner, both = lax.optimization_barrier((corner, both))

    got = [send(corner, [(at(r, c), at(r, c + 4 * d)) for r in every_row for c in (0, 1)]) for d in SHIFTS[1:]]
    parts = [
        send(both[d], [(at(r, c), at(r + 2 * d, c)) for r in (0, 1) for c in every_col])
        for d in SHIFTS[1:]
    ]
    corner = jnp.where(my_col < 2, corner, got[0] + got[1] + got[2])
    block = jnp.where(depth == 0, both[0], parts[0] + parts[1] + parts[2]).reshape(WIDE, BLOCK)
    corner, block = lax.optimization_barrier((corner, block))

    got = [
        send(corner, [(at(r, 4 * x + y), at(r, 4 * x + (y ^ e))) for r in every_row for x in range(4) for y in (0, 1)])
        for e in (1, 2, 3)
    ]
    block_row = send(block, [(at(r, c), at(c % n_row, 2 * r + c // n_row)) for r in every_row for c in every_col])
    y = my_col % 4
    left = jnp.where(y == 0, corner, jnp.where(y == 1, got[0], jnp.where(y == 2, got[1], got[2])))
    right = jnp.where(y == 1, corner, jnp.where(y == 0, got[0], jnp.where(y == 3, got[1], got[2])))
    mine = jnp.stack([left, right])
    mine, block_row, block = lax.optimization_barrier((mine, block_row, block))

    swap = [(at(r, c), at(r + 1 - 2 * (r % 2), c)) for r in every_row for c in every_col]
    other = send(mine, swap)
    turned = turn(block_row)
    line = [turned] + [send(turned, near(1, d)) for d in SHIFTS[1:]]
    tall = [block] + [
        send(block, [(at(r, c), at((r + 2 * d) % n_row, c)) for r in every_row for c in every_col])
        for d in SHIFTS[1:]
    ]
    line = jnp.stack(line)
    tall = jnp.stack(tall)
    mine, other, line, tall = lax.optimization_barrier((mine, other, line, tall))

    row_parts = [line] + [send(line, near(2, d)) for d in SHIFTS[1:]]
    beside = send(tall, swap)
    lower, inverse = head(mine, other)
    return update(lower, inverse, row_parts, [tall, beside], stored)


def solution(mesh):
    body = functools.partial(on_device, n_row=mesh.shape["row"], n_col=mesh.shape["col"])
    return jax.shard_map(
        body,
        mesh=mesh,
        in_specs=(P("row", "col"),),
        out_specs=(P("row", "col"), P("row", None)),
        check_vma=False,
    )
```

```python
import functools

import jax
import jax.numpy as jnp
from jax import lax
from jax.experimental import pallas as pl
from jax.experimental.pallas import tpu as pltpu
from jax.sharding import PartitionSpec as P

BLOCK = 128
WIDE = 2 * BLOCK
GROUP = 8
SHIFTS = (0, 1, 3, 2)
F32 = jnp.float32
BF16 = jnp.bfloat16
AXES = ("row", "col")
NT = (((1,), (1,)), ((), ()))
NN = (((1,), (0,)), ((), ()))


def exact(left, right, dims):
    return lax.dot_general(
        left, right, dims, precision=lax.Precision.HIGHEST, preferred_element_type=F32
    )


def eliminate(matrix):
    lane = lax.broadcasted_iota(jnp.int32, (8, BLOCK), 1)
    sub = lax.broadcasted_iota(jnp.int32, (8, BLOCK), 0)
    rows = [matrix[8 * i : 8 * i + 8, :] for i in range(BLOCK // 8)]
    for first in range(0, BLOCK, GROUP):
        at = first // 8
        cols = {}
        for j in range(GROUP):
            for i in range(at, BLOCK // 8):
                cols[j, i] = jnp.broadcast_to(rows[i][:, first + j : first + j + 1], (8, BLOCK))
        for j in range(GROUP):
            k = first + j
            s = k % 8
            here = lane == k
            pivot = 1.0 / cols[j, at][s : s + 1, :]
            row = jnp.where(here[:1], 1.0, rows[at][s : s + 1, :])
            heads = {m: cols[m, at][s : s + 1, :] for m in range(j + 1, GROUP)}
            for i in range(at, BLOCK // 8):
                factor = cols[j, i] * pivot
                if i == at:
                    factor = jnp.where(sub > s, factor, 0.0)
                    rows[i] = jnp.where(here & (sub > s), 0.0, rows[i]) - factor * row
                else:
                    rows[i] = jnp.where(here, 0.0, rows[i]) - factor * row
                for m in range(j + 1, GROUP):
                    cols[m, i] = cols[m, i] - factor * heads[m]
    return jnp.concatenate(rows, axis=0)


def factor_block(matrix):
    done = eliminate(matrix)
    r = lax.broadcasted_iota(jnp.int32, (BLOCK, BLOCK), 0)
    c = lax.broadcasted_iota(jnp.int32, (BLOCK, BLOCK), 1)
    pivots = jnp.sum(jnp.where(r == c, done, 0.0), axis=1, keepdims=True)
    scale = lax.rsqrt(pivots)
    scale = scale * (1.5 - 0.5 * pivots * scale * scale)
    upper = jnp.where(r <= c, done, 0.0) * scale
    inverse = jnp.where(r > c, done, jnp.where(r == c, 1.0, 0.0)) * scale
    return upper.T, inverse


def head_kernel(mine_ref, other_ref, lower_ref, inverse_ref):
    first = lax.axis_index("row") % 2 == 0
    zero = jnp.zeros((BLOCK, BLOCK), F32)
    l00, i00 = factor_block(jnp.where(first, mine_ref[:, :BLOCK], other_ref[:, :BLOCK]))
    l10 = exact(jnp.where(first, mine_ref[:, BLOCK:], other_ref[:, BLOCK:]), i00, NT)
    rest = jnp.where(first, other_ref[:, BLOCK:], mine_ref[:, BLOCK:]) - exact(l10, l10, NT)
    l11, i11 = factor_block(rest)
    i10 = -exact(i11, exact(l10, i00, NN), NN)
    lower_ref[0, :, :BLOCK] = l00
    lower_ref[0, :, BLOCK:] = zero
    lower_ref[1, :, :BLOCK] = l10
    lower_ref[1, :, BLOCK:] = l11
    inverse_ref[:BLOCK, :BLOCK] = i00
    inverse_ref[:BLOCK, BLOCK:] = zero
    inverse_ref[BLOCK:, :BLOCK] = i10
    inverse_ref[BLOCK:, BLOCK:] = i11


def head(mine, other):
    return pl.pallas_call(
        head_kernel,
        out_shape=(
            jax.ShapeDtypeStruct((2, BLOCK, WIDE), F32),
            jax.ShapeDtypeStruct((WIDE, WIDE), F32),
        ),
        cost_estimate=pl.CostEstimate(flops=10**8, bytes_accessed=10**6, transcendentals=0),
        compiler_params=pltpu.CompilerParams(vmem_limit_bytes=20 * 2**20),
        name="head",
    )(mine, other)


def hold_kernel(stored_ref, held_ref, sem):
    copy = pltpu.make_async_copy(stored_ref, held_ref, sem)
    copy.start()
    copy.wait()


def hold(stored):
    return pl.pallas_call(
        hold_kernel,
        in_specs=[pl.BlockSpec(memory_space=pltpu.HBM)],
        out_specs=pl.BlockSpec(memory_space=pltpu.VMEM),
        out_shape=pltpu.VMEM(stored.shape, F32),
        scratch_shapes=[pltpu.SemaphoreType.DMA(())],
        compiler_params=pltpu.CompilerParams(vmem_limit_bytes=46 * 2**20),
        cost_estimate=pl.CostEstimate(flops=0, bytes_accessed=2**23, transcendentals=0),
        name="hold",
    )(stored)


def open_kernel(stored_ref, strip_ref, keep_ref, give_ref, sem):
    copy = pltpu.make_async_copy(stored_ref.at[pl.ds(0, BLOCK)], strip_ref, sem)
    copy.start()
    first = lax.axis_index("row") % 2 == 0
    last = keep_ref.shape[0] - 1
    copy.wait()
    keep_ref[last] = strip_ref[:, :BLOCK]
    give_ref[last] = strip_ref[:, :BLOCK]
    for b in range(last):
        even = strip_ref[:, 2 * b * BLOCK : (2 * b + 1) * BLOCK]
        odd = strip_ref[:, (2 * b + 1) * BLOCK : (2 * b + 2) * BLOCK]
        keep_ref[b] = jnp.where(first, even, odd).T
        give_ref[b] = jnp.where(first, odd, even).T


def open_strip(stored):
    cols = stored.shape[1]
    part = jax.ShapeDtypeStruct((cols // WIDE + 1, BLOCK, BLOCK), F32)
    return pl.pallas_call(
        open_kernel,
        in_specs=[pl.BlockSpec(memory_space=pl.ANY)],
        out_shape=(jax.ShapeDtypeStruct((BLOCK, cols), F32), part, part),
        scratch_shapes=[pltpu.SemaphoreType.DMA(())],
        name="open",
    )(stored)


def pack_kernel(keep_ref, other_ref, *out_refs):
    first = lax.axis_index("row") % 2 == 0
    last = keep_ref.shape[0] - 1
    for b, out_ref in enumerate(out_refs):
        for n, t in enumerate((b, last)):
            out_ref[:, 2 * n * BLOCK : (2 * n + 1) * BLOCK] = jnp.where(first, keep_ref[t], other_ref[t])
            out_ref[:, (2 * n + 1) * BLOCK : (2 * n + 2) * BLOCK] = jnp.where(first, other_ref[t], keep_ref[t])


def pack(keep, other):
    count = keep.shape[0] - 1
    return pl.pallas_call(
        pack_kernel, out_shape=(jax.ShapeDtypeStruct((BLOCK, 2 * WIDE), F32),) * count, name="pack"
    )(keep, other)


def split(x):
    high = x.astype(BF16)
    return high, (x - high.astype(F32)).astype(BF16)


def update_kernel(
    lower_ref, inverse_ref, row0_ref, row1_ref, row2_ref, row3_ref, tall_ref, beside_ref, a_ref, out_ref, factor_ref,
    a_buf, row_buf, factor_buf, col_buf, right_ref, row_sem, col_sem, out_sem, factor_sem,
):
    my_row = lax.axis_index("row")
    my_col = lax.axis_index("col")
    x, y = my_col // 4, my_col % 4
    even = my_row % 2 == 0
    count, _, cols = a_ref.shape
    blocks = cols // BLOCK

    place = []
    for far in SHIFTS:
        for near in SHIFTS:
            dx = jnp.where(even, far, near)
            dy = jnp.where(even, near, far)
            place.append((x - dx + 4) % 4 * 4 + (y - dy + 4) % 4)

    def start(src, dst, sem):
        copy = pltpu.make_async_copy(src, dst, sem)
        copy.start()
        return copy

    core = my_row % 2
    col_in = [
        start(tall_ref, col_buf.at[core], col_sem.at[0]),
        start(beside_ref, col_buf.at[1 - core], col_sem.at[1]),
    ]
    row_in = [
        start(ref, row_buf.at[a], row_sem.at[a])
        for a, ref in enumerate((row0_ref, row1_ref, row2_ref, row3_ref))
    ]

    high, low = split(inverse_ref[...])
    by_left = jnp.concatenate([high, high, low], axis=1)
    by_right = jnp.concatenate([high, low, high], axis=1)
    for copy in col_in:
        copy.wait()
    for b in range(0, blocks, 2):
        span = slice(b * BLOCK, (b + 2) * BLOCK)
        high, low = split(jnp.concatenate([col_buf[0, :, span], col_buf[1, :, span]], axis=0))
        stack = jnp.concatenate([high, low, high], axis=0)
        part = lax.dot_general(by_left, stack, NN, preferred_element_type=F32)
        if b == 0:
            known = jnp.concatenate([lower_ref[jnp.minimum(my_col, 1)].T, part[:, BLOCK:]], axis=1)
            part = jnp.where(my_col < 2, known, part)
        high, low = split(part)
        right_ref[0:WIDE, span] = high
        right_ref[WIDE : 2 * WIDE, span] = low
        right_ref[2 * WIDE : 3 * WIDE, span] = high

    out = []
    for a in range(4):
        row_in[a].wait()
        high, low = split(row_buf[a].reshape(4 * BLOCK, WIDE))
        left = jnp.concatenate([high, high, low], axis=1)
        part = lax.dot_general(left, by_right, NT, preferred_element_type=F32)
        factor_buf[a] = part.reshape(4, BLOCK, WIDE)
        for s in range(4):
            t = 4 * a + s

            @pl.when((my_row < 2) & (place[t] == 0))
            def _():
                factor_buf[a, s] = lower_ref[jnp.minimum(my_row, 1)]

        for s in range(4):
            t = 4 * a + s
            out.append(start(factor_buf.at[a, s], factor_ref.at[place[t]], factor_sem.at[t]))
        high, low = split(factor_buf[a].reshape(4 * BLOCK, WIDE))
        left = jnp.concatenate([high, high, low], axis=1)
        for n in range(0, cols, WIDE):
            span = slice(n, n + WIDE)
            part = lax.dot_general(left, right_ref[:, span], NN, preferred_element_type=F32)
            for s in range(4):
                t = 4 * a + s
                a_buf[t, :, span] = a_ref[place[t], :, span] - part[s * BLOCK : (s + 1) * BLOCK]
        for s in range(4):
            t = 4 * a + s
            out.append(start(a_buf.at[t], out_ref.at[place[t]], out_sem.at[t]))
    for copy in out:
        copy.wait()


def update(lower, inverse, row_parts, col_parts, held):
    count, _, cols = held.shape
    rows = count * BLOCK
    here = pl.BlockSpec(memory_space=pltpu.VMEM)
    there = pl.BlockSpec(memory_space=pltpu.HBM)
    trailing, factor = pl.pallas_call(
        update_kernel,
        in_specs=[here] * 2 + [there] * 6 + [here],
        out_specs=[there] * 2,
        out_shape=(
            jax.ShapeDtypeStruct((count, BLOCK, cols), F32),
            jax.ShapeDtypeStruct((count, BLOCK, WIDE), F32),
        ),
        scratch_shapes=[
            pltpu.VMEM((count, BLOCK, cols), F32),
            pltpu.VMEM((4, 4, BLOCK, WIDE), F32),
            pltpu.VMEM((4, 4, BLOCK, WIDE), F32),
            pltpu.VMEM((2, BLOCK, cols), F32),
            pltpu.VMEM((3 * WIDE, cols), BF16),
            pltpu.SemaphoreType.DMA((4,)),
            pltpu.SemaphoreType.DMA((2,)),
            pltpu.SemaphoreType.DMA((count,)),
            pltpu.SemaphoreType.DMA((count,)),
        ],
        compiler_params=pltpu.CompilerParams(vmem_limit_bytes=30 * 2**20),
        name="update",
    )(lower, inverse, *row_parts, *col_parts, held)
    return trailing.reshape(rows, cols), factor.reshape(rows, WIDE)


def on_device(stored, n_row, n_col):
    my_row = lax.axis_index("row")
    my_col = lax.axis_index("col")
    core = my_row % 2
    depth = my_row // 2

    def at(r, c):
        return r * n_col + c

    def send(x, pairs):
        return lax.ppermute(x, AXES, pairs)

    def near(phase, d):
        pairs = []
        for r in range(n_row):
            for c in range(n_col):
                x, y = divmod(c, 4)
                if (r % 2 == 0) == (phase == 1):
                    pairs.append((at(r, c), at(r, x * 4 + (y + d) % 4)))
                else:
                    pairs.append((at(r, c), at(r, (x + d) % 4 * 4 + y)))
        return pairs

    every_row, every_col = range(n_row), range(n_col)

    strip, keep, give = open_strip(stored)
    other = send(give, [(at(r, c), at(1 - r, c)) for r in (0, 1) for c in every_col])
    tall = send(strip, [(at(r, c), at(r + 4, c)) for r in (0, 1) for c in every_col])
    messages = pack(keep, other)

    parts = [
        send(
            message,
            [(at(r, c), at(c % n_row, 2 * (2 * b + r) + c // n_row)) for r in (0, 1) for c in every_col],
        )
        for b, message in enumerate(messages)
    ]
    total = parts[0] + parts[1] + parts[2] + parts[3]
    block, corner = total[:, :WIDE], total[:, WIDE:]
    block, corner = lax.optimization_barrier((block, corner))

    near_y = [4 * x + y for x in range(4) for y in (0, 2)]
    got = send(corner, [(at(r, c), at(r + 4, c)) for r in (0, 1) for c in near_y])
    line = [block] + [send(block, near(1, d)) for d in SHIFTS[1:]]
    corner = jnp.where(depth == 0, corner, got)
    got = send(corner, [(at(r, c), at((r + 6) % n_row, c)) for r in (0, 1, 4, 5) for c in near_y])
    corner = jnp.where(depth % 2 == 0, corner, got)
    got = send(corner, [(at(r, c), at(r, c + 1)) for r in every_row for c in near_y])
    corner = jnp.where(my_col % 2 == 0, corner, got)
    line = jnp.stack(line)
    corner, line, tall = lax.optimization_barrier((corner, line, tall))

    row_parts = [line] + [send(line, near(2, d)) for d in SHIFTS[1:]]
    tall = jnp.where(depth == 0, strip, tall)
    got_tall = send(tall, [(at(r, c), at(r + 2, c)) for r in (0, 1, 4, 5) for c in every_col])
    swap = [(at(r, c), at(r + 1 - 2 * (r % 2), c)) for r in every_row for c in every_col]
    other = send(corner, swap)
    lower, inverse = head(corner, other)
    inverse, got_tall, tall, stored = lax.optimization_barrier((inverse, got_tall, tall, stored))

    tall = jnp.where(depth % 2 == 0, tall, got_tall)
    beside = send(tall, swap)
    held = hold(stored.reshape(-1, BLOCK, stored.shape[1]))
    return update(lower, inverse, row_parts, [tall, beside], held)


def solution(mesh):
    body = functools.partial(on_device, n_row=mesh.shape["row"], n_col=mesh.shape["col"])
    return jax.shard_map(
        body,
        mesh=mesh,
        in_specs=(P("row", "col"),),
        out_specs=(P("row", "col"), P("row", None)),
        check_vma=False,
    )
```

```python
import functools

import jax
import jax.numpy as jnp
from jax import lax
from jax.experimental import pallas as pl
from jax.experimental.pallas import tpu as pltpu
from jax.sharding import PartitionSpec as P

BLOCK = 128
WIDE = 2 * BLOCK
GROUP = 8
SHIFTS = (0, 1, 3, 2)
F32 = jnp.float32
BF16 = jnp.bfloat16
AXES = ("row", "col")
NT = (((1,), (1,)), ((), ()))
NN = (((1,), (0,)), ((), ()))


def exact(left, right, dims):
    return lax.dot_general(
        left, right, dims, precision=lax.Precision.HIGHEST, preferred_element_type=F32
    )


def eliminate(matrix):
    lane = lax.broadcasted_iota(jnp.int32, (8, BLOCK), 1)
    sub = lax.broadcasted_iota(jnp.int32, (8, BLOCK), 0)
    rows = [matrix[8 * i : 8 * i + 8, :] for i in range(BLOCK // 8)]
    for first in range(0, BLOCK, GROUP):
        at = first // 8
        cols = {}
        for j in range(GROUP):
            for i in range(at, BLOCK // 8):
                cols[j, i] = jnp.broadcast_to(rows[i][:, first + j : first + j + 1], (8, BLOCK))
        for j in range(GROUP):
            k = first + j
            s = k % 8
            here = lane == k
            pivot = 1.0 / cols[j, at][s : s + 1, :]
            row = jnp.where(here[:1], 1.0, rows[at][s : s + 1, :])
            heads = {m: cols[m, at][s : s + 1, :] for m in range(j + 1, GROUP)}
            for i in range(at, BLOCK // 8):
                factor = cols[j, i] * pivot
                if i == at:
                    factor = jnp.where(sub > s, factor, 0.0)
                    rows[i] = jnp.where(here & (sub > s), 0.0, rows[i]) - factor * row
                else:
                    rows[i] = jnp.where(here, 0.0, rows[i]) - factor * row
                for m in range(j + 1, GROUP):
                    cols[m, i] = cols[m, i] - factor * heads[m]
    return jnp.concatenate(rows, axis=0)


def factor_block(matrix):
    done = eliminate(matrix)
    r = lax.broadcasted_iota(jnp.int32, (BLOCK, BLOCK), 0)
    c = lax.broadcasted_iota(jnp.int32, (BLOCK, BLOCK), 1)
    pivots = jnp.sum(jnp.where(r == c, done, 0.0), axis=1, keepdims=True)
    scale = lax.rsqrt(pivots)
    scale = scale * (1.5 - 0.5 * pivots * scale * scale)
    upper = jnp.where(r <= c, done, 0.0) * scale
    inverse = jnp.where(r > c, done, jnp.where(r == c, 1.0, 0.0)) * scale
    return upper.T, inverse


def head_kernel(mine_ref, other_ref, lower_ref, inverse_ref):
    first = lax.axis_index("row") % 2 == 0
    zero = jnp.zeros((BLOCK, BLOCK), F32)
    l00, i00 = factor_block(jnp.where(first, mine_ref[:, :BLOCK], other_ref[:, :BLOCK]))
    l10 = exact(jnp.where(first, mine_ref[:, BLOCK:], other_ref[:, BLOCK:]), i00, NT)
    rest = jnp.where(first, other_ref[:, BLOCK:], mine_ref[:, BLOCK:]) - exact(l10, l10, NT)
    l11, i11 = factor_block(rest)
    i10 = -exact(i11, exact(l10, i00, NN), NN)
    lower_ref[0, :, :BLOCK] = l00
    lower_ref[0, :, BLOCK:] = zero
    lower_ref[1, :, :BLOCK] = l10
    lower_ref[1, :, BLOCK:] = l11
    inverse_ref[:BLOCK, :BLOCK] = i00
    inverse_ref[:BLOCK, BLOCK:] = zero
    inverse_ref[BLOCK:, :BLOCK] = i10
    inverse_ref[BLOCK:, BLOCK:] = i11


def head(mine, other):
    return pl.pallas_call(
        head_kernel,
        out_shape=(
            jax.ShapeDtypeStruct((2, BLOCK, WIDE), F32),
            jax.ShapeDtypeStruct((WIDE, WIDE), F32),
        ),
        cost_estimate=pl.CostEstimate(flops=10**8, bytes_accessed=10**6, transcendentals=0),
        compiler_params=pltpu.CompilerParams(vmem_limit_bytes=20 * 2**20),
        name="head",
    )(mine, other)


def hold_kernel(stored_ref, held_ref, sem):
    copy = pltpu.make_async_copy(stored_ref, held_ref, sem)
    copy.start()
    copy.wait()


def hold(stored):
    return pl.pallas_call(
        hold_kernel,
        in_specs=[pl.BlockSpec(memory_space=pltpu.HBM)],
        out_specs=pl.BlockSpec(memory_space=pltpu.VMEM),
        out_shape=pltpu.VMEM(stored.shape, F32),
        scratch_shapes=[pltpu.SemaphoreType.DMA(())],
        compiler_params=pltpu.CompilerParams(vmem_limit_bytes=46 * 2**20),
        cost_estimate=pl.CostEstimate(flops=0, bytes_accessed=2**23, transcendentals=0),
        name="hold",
    )(stored)


def open_kernel(stored_ref, strip_ref, corner_ref, keep_ref, give_ref, sem):
    copy = pltpu.make_async_copy(stored_ref.at[pl.ds(0, BLOCK)], strip_ref, sem)
    copy.start()
    first = lax.axis_index("row") % 2 == 0
    copy.wait()
    corner_ref[...] = strip_ref[:, :BLOCK]
    for b in range(keep_ref.shape[0]):
        even = strip_ref[:, 2 * b * BLOCK : (2 * b + 1) * BLOCK]
        odd = strip_ref[:, (2 * b + 1) * BLOCK : (2 * b + 2) * BLOCK]
        keep_ref[b] = jnp.where(first, even, odd).T
        give_ref[b] = jnp.where(first, odd, even).T


def open_strip(stored):
    cols = stored.shape[1]
    one = jax.ShapeDtypeStruct((BLOCK, BLOCK), F32)
    part = jax.ShapeDtypeStruct((cols // WIDE, BLOCK, BLOCK), F32)
    return pl.pallas_call(
        open_kernel,
        in_specs=[pl.BlockSpec(memory_space=pl.ANY)],
        out_shape=(jax.ShapeDtypeStruct((BLOCK, cols), F32), one, part, part),
        scratch_shapes=[pltpu.SemaphoreType.DMA(())],
        name="open",
    )(stored)


def pack_kernel(keep_ref, other_ref, corner_ref, beside_ref, *out_refs):
    first = lax.axis_index("row") % 2 == 0
    upper = jnp.where(first, corner_ref[...], beside_ref[...])
    lower = jnp.where(first, beside_ref[...], corner_ref[...])
    for b, out_ref in enumerate(out_refs):
        out_ref[:, :BLOCK] = jnp.where(first, keep_ref[b], other_ref[b])
        out_ref[:, BLOCK:WIDE] = jnp.where(first, other_ref[b], keep_ref[b])
        out_ref[:, WIDE : WIDE + BLOCK] = upper
        out_ref[:, WIDE + BLOCK :] = lower


def pack(keep, other, corner, beside):
    return pl.pallas_call(
        pack_kernel,
        out_shape=(jax.ShapeDtypeStruct((BLOCK, 2 * WIDE), F32),) * keep.shape[0],
        name="pack",
    )(keep, other, corner, beside)


def split(x):
    high = x.astype(BF16)
    return high, (x - high.astype(F32)).astype(BF16)


def update_kernel(
    lower_ref, inverse_ref, row0_ref, row1_ref, row2_ref, row3_ref, tall_ref, beside_ref, a_ref, out_ref, factor_ref,
    a_buf, row_buf, factor_buf, col_buf, right_ref, row_sem, col_sem, out_sem, factor_sem,
):
    my_row = lax.axis_index("row")
    my_col = lax.axis_index("col")
    x, y = my_col // 4, my_col % 4
    even = my_row % 2 == 0
    count, _, cols = a_ref.shape
    blocks = cols // BLOCK

    place = []
    for far in SHIFTS:
        for near in SHIFTS:
            dx = jnp.where(even, far, near)
            dy = jnp.where(even, near, far)
            place.append((x - dx + 4) % 4 * 4 + (y - dy + 4) % 4)

    def start(src, dst, sem):
        copy = pltpu.make_async_copy(src, dst, sem)
        copy.start()
        return copy

    core = my_row % 2
    col_in = [
        start(tall_ref, col_buf.at[core], col_sem.at[0]),
        start(beside_ref, col_buf.at[1 - core], col_sem.at[1]),
    ]
    row_in = [
        start(ref, row_buf.at[a], row_sem.at[a])
        for a, ref in enumerate((row0_ref, row1_ref, row2_ref, row3_ref))
    ]

    high, low = split(inverse_ref[...])
    by_left = jnp.concatenate([high, high, low], axis=1)
    by_right = jnp.concatenate([high, low, high], axis=1)
    for copy in col_in:
        copy.wait()
    for b in range(0, blocks, 2):
        span = slice(b * BLOCK, (b + 2) * BLOCK)
        high, low = split(jnp.concatenate([col_buf[0, :, span], col_buf[1, :, span]], axis=0))
        stack = jnp.concatenate([high, low, high], axis=0)
        part = lax.dot_general(by_left, stack, NN, preferred_element_type=F32)
        if b == 0:
            known = jnp.concatenate([lower_ref[jnp.minimum(my_col, 1)].T, part[:, BLOCK:]], axis=1)
            part = jnp.where(my_col < 2, known, part)
        high, low = split(part)
        right_ref[0:WIDE, span] = high
        right_ref[WIDE : 2 * WIDE, span] = low
        right_ref[2 * WIDE : 3 * WIDE, span] = high

    out = []
    for a in range(4):
        row_in[a].wait()
        high, low = split(row_buf[a].reshape(4 * BLOCK, WIDE))
        left = jnp.concatenate([high, high, low], axis=1)
        part = lax.dot_general(left, by_right, NT, preferred_element_type=F32)
        factor_buf[a] = part.reshape(4, BLOCK, WIDE)
        for s in range(4):
            t = 4 * a + s

            @pl.when((my_row < 2) & (place[t] == 0))
            def _():
                factor_buf[a, s] = lower_ref[jnp.minimum(my_row, 1)]

        for s in range(4):
            t = 4 * a + s
            out.append(start(factor_buf.at[a, s], factor_ref.at[place[t]], factor_sem.at[t]))
        high, low = split(factor_buf[a].reshape(4 * BLOCK, WIDE))
        left = jnp.concatenate([high, high, low], axis=1)
        for n in range(0, cols, WIDE):
            span = slice(n, n + WIDE)
            part = lax.dot_general(left, right_ref[:, span], NN, preferred_element_type=F32)
            for s in range(4):
                t = 4 * a + s
                a_buf[t, :, span] = a_ref[place[t], :, span] - part[s * BLOCK : (s + 1) * BLOCK]
        for s in range(4):
            t = 4 * a + s
            out.append(start(a_buf.at[t], out_ref.at[place[t]], out_sem.at[t]))
    for copy in out:
        copy.wait()


def update(lower, inverse, row_parts, col_parts, held):
    count, _, cols = held.shape
    rows = count * BLOCK
    here = pl.BlockSpec(memory_space=pltpu.VMEM)
    there = pl.BlockSpec(memory_space=pltpu.HBM)
    trailing, factor = pl.pallas_call(
        update_kernel,
        in_specs=[here] * 2 + [there] * 6 + [here],
        out_specs=[there] * 2,
        out_shape=(
            jax.ShapeDtypeStruct((count, BLOCK, cols), F32),
            jax.ShapeDtypeStruct((count, BLOCK, WIDE), F32),
        ),
        scratch_shapes=[
            pltpu.VMEM((count, BLOCK, cols), F32),
            pltpu.VMEM((4, 4, BLOCK, WIDE), F32),
            pltpu.VMEM((4, 4, BLOCK, WIDE), F32),
            pltpu.VMEM((2, BLOCK, cols), F32),
            pltpu.VMEM((3 * WIDE, cols), BF16),
            pltpu.SemaphoreType.DMA((4,)),
            pltpu.SemaphoreType.DMA((2,)),
            pltpu.SemaphoreType.DMA((count,)),
            pltpu.SemaphoreType.DMA((count,)),
        ],
        compiler_params=pltpu.CompilerParams(vmem_limit_bytes=30 * 2**20),
        name="update",
    )(lower, inverse, *row_parts, *col_parts, held)
    return trailing.reshape(rows, cols), factor.reshape(rows, WIDE)


def on_device(stored, n_row, n_col):
    my_row = lax.axis_index("row")
    my_col = lax.axis_index("col")
    core = my_row % 2
    depth = my_row // 2

    def at(r, c):
        return r * n_col + c

    def send(x, pairs):
        return lax.ppermute(x, AXES, pairs)

    def near(phase, d):
        pairs = []
        for r in range(n_row):
            for c in range(n_col):
                x, y = divmod(c, 4)
                if (r % 2 == 0) == (phase == 1):
                    pairs.append((at(r, c), at(r, x * 4 + (y + d) % 4)))
                else:
                    pairs.append((at(r, c), at(r, (x + d) % 4 * 4 + y)))
        return pairs

    every_row, every_col = range(n_row), range(n_col)

    strip, corner, keep, give = open_strip(stored)
    other = send(give, [(at(r, c), at(1 - r, c)) for r in (0, 1) for c in every_col])
    got = send(corner, [(at(r, c), at(r, c + 4)) for r in (0, 1) for c in (0, 1)])
    corner = jnp.where(my_col < 4, corner, got)
    got = send(corner, [(at(r, c), at(1 - r, c)) for r in (0, 1) for c in (0, 1, 4, 5)])
    tall = send(strip, [(at(r, c), at(r + 4, c)) for r in (0, 1) for c in every_col])
    messages = pack(keep, other, corner, got)

    parts = [
        send(
            message,
            [(at(r, c), at(c % n_row, 2 * (2 * b + r) + c // n_row)) for r in (0, 1) for c in every_col],
        )
        for b, message in enumerate(messages)
    ]
    total = parts[0] + parts[1] + parts[2] + parts[3]
    block, corner = total[:, :WIDE], total[:, WIDE:]
    block, corner = lax.optimization_barrier((block, corner))

    near_y = [4 * x + y for x in range(4) for y in (0, 2)]
    got = send(corner, [(at(r, c), at((r + 6) % n_row, c)) for r in (0, 1, 4, 5) for c in near_y])
    line = [block] + [send(block, near(1, d)) for d in SHIFTS[1:]]
    corner = jnp.where(depth % 2 == 0, corner, got)
    corner, tall = lax.optimization_barrier((corner, tall))
    tall = jnp.where(depth == 0, strip, tall)
    got_tall = send(tall, [(at(r, c), at(r + 2, c)) for r in (0, 1, 4, 5) for c in every_col])
    got = send(corner, [(at(r, c), at(r, c + 1)) for r in every_row for c in near_y])
    corner = jnp.where(my_col % 2 == 0, corner, got)
    line = jnp.stack(line)
    corner, line = lax.optimization_barrier((corner, line))

    row_parts = [line] + [send(line, near(2, d)) for d in SHIFTS[1:]]
    swap = [(at(r, c), at(r + 1 - 2 * (r % 2), c)) for r in every_row for c in every_col]
    other = send(corner, swap)
    lower, inverse = head(corner, other)
    inverse, got_tall, tall, stored = lax.optimization_barrier((inverse, got_tall, tall, stored))

    tall = jnp.where(depth % 2 == 0, tall, got_tall)
    beside = send(tall, swap)
    held = hold(stored.reshape(-1, BLOCK, stored.shape[1]))
    return update(lower, inverse, row_parts, [tall, beside], held)


def solution(mesh):
    body = functools.partial(on_device, n_row=mesh.shape["row"], n_col=mesh.shape["col"])
    return jax.shard_map(
        body,
        mesh=mesh,
        in_specs=(P("row", "col"),),
        out_specs=(P("row", "col"), P("row", None)),
        check_vma=False,
    )
```

```python
import functools

import jax
import jax.numpy as jnp
from jax import lax
from jax.experimental import pallas as pl
from jax.experimental.pallas import tpu as pltpu
from jax.sharding import PartitionSpec as P

BLOCK = 128
WIDE = 2 * BLOCK
GROUP = 8
SHIFTS = (0, 1, 3, 2)
F32 = jnp.float32
BF16 = jnp.bfloat16
AXES = ("row", "col")
NT = (((1,), (1,)), ((), ()))
NN = (((1,), (0,)), ((), ()))


def exact(left, right, dims):
    return lax.dot_general(
        left, right, dims, precision=lax.Precision.HIGHEST, preferred_element_type=F32
    )


def eliminate(matrix):
    lane = lax.broadcasted_iota(jnp.int32, (8, BLOCK), 1)
    sub = lax.broadcasted_iota(jnp.int32, (8, BLOCK), 0)
    rows = [matrix[8 * i : 8 * i + 8, :] for i in range(BLOCK // 8)]
    for first in range(0, BLOCK, GROUP):
        at = first // 8
        cols = {}
        for j in range(GROUP):
            for i in range(at, BLOCK // 8):
                cols[j, i] = jnp.broadcast_to(rows[i][:, first + j : first + j + 1], (8, BLOCK))
        for j in range(GROUP):
            k = first + j
            s = k % 8
            here = lane == k
            pivot = 1.0 / cols[j, at][s : s + 1, :]
            row = jnp.where(here[:1], 1.0, rows[at][s : s + 1, :])
            heads = {m: cols[m, at][s : s + 1, :] for m in range(j + 1, GROUP)}
            for i in range(at, BLOCK // 8):
                factor = cols[j, i] * pivot
                if i == at:
                    factor = jnp.where(sub > s, factor, 0.0)
                    rows[i] = jnp.where(here & (sub > s), 0.0, rows[i]) - factor * row
                else:
                    rows[i] = jnp.where(here, 0.0, rows[i]) - factor * row
                for m in range(j + 1, GROUP):
                    cols[m, i] = cols[m, i] - factor * heads[m]
    return jnp.concatenate(rows, axis=0)


def factor_block(matrix):
    done = eliminate(matrix)
    r = lax.broadcasted_iota(jnp.int32, (BLOCK, BLOCK), 0)
    c = lax.broadcasted_iota(jnp.int32, (BLOCK, BLOCK), 1)
    pivots = jnp.sum(jnp.where(r == c, done, 0.0), axis=1, keepdims=True)
    scale = lax.rsqrt(pivots)
    scale = scale * (1.5 - 0.5 * pivots * scale * scale)
    upper = jnp.where(r <= c, done, 0.0) * scale
    inverse = jnp.where(r > c, done, jnp.where(r == c, 1.0, 0.0)) * scale
    return upper.T, inverse


def head_kernel(mine_ref, other_ref, lower_ref, inverse_ref):
    first = lax.axis_index("row") % 2 == 0
    zero = jnp.zeros((BLOCK, BLOCK), F32)
    l00, i00 = factor_block(jnp.where(first, mine_ref[:, :BLOCK], other_ref[:, :BLOCK]))
    l10 = exact(jnp.where(first, mine_ref[:, BLOCK:], other_ref[:, BLOCK:]), i00, NT)
    rest = jnp.where(first, other_ref[:, BLOCK:], mine_ref[:, BLOCK:]) - exact(l10, l10, NT)
    l11, i11 = factor_block(rest)
    i10 = -exact(i11, exact(l10, i00, NN), NN)
    lower_ref[0, :, :BLOCK] = l00
    lower_ref[0, :, BLOCK:] = zero
    lower_ref[1, :, :BLOCK] = l10
    lower_ref[1, :, BLOCK:] = l11
    inverse_ref[:BLOCK, :BLOCK] = i00
    inverse_ref[:BLOCK, BLOCK:] = zero
    inverse_ref[BLOCK:, :BLOCK] = i10
    inverse_ref[BLOCK:, BLOCK:] = i11


def head(mine, other):
    return pl.pallas_call(
        head_kernel,
        out_shape=(
            jax.ShapeDtypeStruct((2, BLOCK, WIDE), F32),
            jax.ShapeDtypeStruct((WIDE, WIDE), F32),
        ),
        cost_estimate=pl.CostEstimate(flops=10**8, bytes_accessed=10**6, transcendentals=0),
        compiler_params=pltpu.CompilerParams(vmem_limit_bytes=20 * 2**20),
        name="head",
    )(mine, other)


def hold_kernel(stored_ref, held_ref, sem):
    copy = pltpu.make_async_copy(stored_ref, held_ref, sem)
    copy.start()
    copy.wait()


def hold(stored):
    return pl.pallas_call(
        hold_kernel,
        in_specs=[pl.BlockSpec(memory_space=pltpu.HBM)],
        out_specs=pl.BlockSpec(memory_space=pltpu.VMEM),
        out_shape=pltpu.VMEM(stored.shape, F32),
        scratch_shapes=[pltpu.SemaphoreType.DMA(())],
        compiler_params=pltpu.CompilerParams(vmem_limit_bytes=46 * 2**20),
        cost_estimate=pl.CostEstimate(flops=0, bytes_accessed=2**23, transcendentals=0),
        name="hold",
    )(stored)


def open_kernel(stored_ref, strip_ref, corner_ref, keep_ref, give_ref, sem):
    copy = pltpu.make_async_copy(stored_ref.at[pl.ds(0, BLOCK)], strip_ref, sem)
    copy.start()
    first = lax.axis_index("row") % 2 == 0
    copy.wait()
    corner_ref[...] = strip_ref[:, :BLOCK]
    for b in range(keep_ref.shape[0]):
        even = strip_ref[:, 2 * b * BLOCK : (2 * b + 1) * BLOCK]
        odd = strip_ref[:, (2 * b + 1) * BLOCK : (2 * b + 2) * BLOCK]
        keep_ref[b] = jnp.where(first, even, odd).T
        give_ref[b] = jnp.where(first, odd, even).T


def open_strip(stored):
    cols = stored.shape[1]
    one = jax.ShapeDtypeStruct((BLOCK, BLOCK), F32)
    part = jax.ShapeDtypeStruct((cols // WIDE, BLOCK, BLOCK), F32)
    return pl.pallas_call(
        open_kernel,
        in_specs=[pl.BlockSpec(memory_space=pl.ANY)],
        out_shape=(jax.ShapeDtypeStruct((BLOCK, cols), F32), one, part, part),
        scratch_shapes=[pltpu.SemaphoreType.DMA(())],
        name="open",
    )(stored)


def pack_kernel(keep_ref, other_ref, corner_ref, beside_ref, *out_refs):
    first = lax.axis_index("row") % 2 == 0
    upper = jnp.where(first, corner_ref[...], beside_ref[...])
    lower = jnp.where(first, beside_ref[...], corner_ref[...])
    for b, out_ref in enumerate(out_refs):
        out_ref[:, :BLOCK] = jnp.where(first, keep_ref[b], other_ref[b])
        out_ref[:, BLOCK:WIDE] = jnp.where(first, other_ref[b], keep_ref[b])
        out_ref[:, WIDE : WIDE + BLOCK] = upper
        out_ref[:, WIDE + BLOCK :] = lower


def pack(keep, other, corner, beside):
    return pl.pallas_call(
        pack_kernel,
        out_shape=(jax.ShapeDtypeStruct((BLOCK, 2 * WIDE), F32),) * keep.shape[0],
        name="pack",
    )(keep, other, corner, beside)


def split(x):
    high = x.astype(BF16)
    return high, (x - high.astype(F32)).astype(BF16)


def update_kernel(
    lower_ref, inverse_ref, row0_ref, row1_ref, row2_ref, row3_ref, tall_ref, beside_ref, a_ref, out_ref, factor_ref,
    a_buf, row_buf, factor_buf, col_buf, right_ref, row_sem, col_sem, out_sem, factor_sem,
):
    my_row = lax.axis_index("row")
    my_col = lax.axis_index("col")
    x, y = my_col // 4, my_col % 4
    even = my_row % 2 == 0
    count, _, cols = a_ref.shape
    blocks = cols // BLOCK

    place = []
    for far in SHIFTS:
        for near in SHIFTS:
            dx = jnp.where(even, far, near)
            dy = jnp.where(even, near, far)
            place.append((x - dx + 4) % 4 * 4 + (y - dy + 4) % 4)

    def start(src, dst, sem):
        copy = pltpu.make_async_copy(src, dst, sem)
        copy.start()
        return copy

    core = my_row % 2
    col_in = [
        start(tall_ref, col_buf.at[core], col_sem.at[0]),
        start(beside_ref, col_buf.at[1 - core], col_sem.at[1]),
    ]
    row_in = [
        start(ref, row_buf.at[a], row_sem.at[a])
        for a, ref in enumerate((row0_ref, row1_ref, row2_ref, row3_ref))
    ]

    high, low = split(inverse_ref[...])
    by_left = jnp.concatenate([high, high, low], axis=1)
    by_right = jnp.concatenate([high, low, high], axis=1)
    for copy in col_in:
        copy.wait()
    for b in range(0, blocks, 2):
        span = slice(b * BLOCK, (b + 2) * BLOCK)
        high, low = split(jnp.concatenate([col_buf[0, :, span], col_buf[1, :, span]], axis=0))
        stack = jnp.concatenate([high, low, high], axis=0)
        part = lax.dot_general(by_left, stack, NN, preferred_element_type=F32)
        if b == 0:
            known = jnp.concatenate([lower_ref[jnp.minimum(my_col, 1)].T, part[:, BLOCK:]], axis=1)
            part = jnp.where(my_col < 2, known, part)
        high, low = split(part)
        right_ref[0:WIDE, span] = high
        right_ref[WIDE : 2 * WIDE, span] = low
        right_ref[2 * WIDE : 3 * WIDE, span] = high

    out = []
    for a in range(4):
        row_in[a].wait()
        high, low = split(row_buf[a].reshape(4 * BLOCK, WIDE))
        left = jnp.concatenate([high, high, low], axis=1)
        part = lax.dot_general(left, by_right, NT, preferred_element_type=F32)
        factor_buf[a] = part.reshape(4, BLOCK, WIDE)
        for s in range(4):
            t = 4 * a + s

            @pl.when((my_row < 2) & (place[t] == 0))
            def _():
                factor_buf[a, s] = lower_ref[jnp.minimum(my_row, 1)]

        for s in range(4):
            t = 4 * a + s
            out.append(start(factor_buf.at[a, s], factor_ref.at[place[t]], factor_sem.at[t]))
        high, low = split(factor_buf[a].reshape(4 * BLOCK, WIDE))
        left = jnp.concatenate([high, high, low], axis=1)
        for n in range(0, cols, WIDE):
            span = slice(n, n + WIDE)
            part = lax.dot_general(left, right_ref[:, span], NN, preferred_element_type=F32)
            for s in range(4):
                t = 4 * a + s
                a_buf[t, :, span] = a_ref[place[t], :, span] - part[s * BLOCK : (s + 1) * BLOCK]
        for s in range(4):
            t = 4 * a + s
            out.append(start(a_buf.at[t], out_ref.at[place[t]], out_sem.at[t]))
    for copy in out:
        copy.wait()


def update(lower, inverse, row_parts, col_parts, held):
    count, _, cols = held.shape
    rows = count * BLOCK
    here = pl.BlockSpec(memory_space=pltpu.VMEM)
    there = pl.BlockSpec(memory_space=pltpu.HBM)
    trailing, factor = pl.pallas_call(
        update_kernel,
        in_specs=[here] * 2 + [there] * 6 + [here],
        out_specs=[there] * 2,
        out_shape=(
            jax.ShapeDtypeStruct((count, BLOCK, cols), F32),
            jax.ShapeDtypeStruct((count, BLOCK, WIDE), F32),
        ),
        scratch_shapes=[
            pltpu.VMEM((count, BLOCK, cols), F32),
            pltpu.VMEM((4, 4, BLOCK, WIDE), F32),
            pltpu.VMEM((4, 4, BLOCK, WIDE), F32),
            pltpu.VMEM((2, BLOCK, cols), F32),
            pltpu.VMEM((3 * WIDE, cols), BF16),
            pltpu.SemaphoreType.DMA((4,)),
            pltpu.SemaphoreType.DMA((2,)),
            pltpu.SemaphoreType.DMA((count,)),
            pltpu.SemaphoreType.DMA((count,)),
        ],
        compiler_params=pltpu.CompilerParams(vmem_limit_bytes=30 * 2**20),
        name="update",
    )(lower, inverse, *row_parts, *col_parts, held)
    return trailing.reshape(rows, cols), factor.reshape(rows, WIDE)


def on_device(stored, n_row, n_col):
    my_row = lax.axis_index("row")
    my_col = lax.axis_index("col")
    core = my_row % 2
    depth = my_row // 2

    def at(r, c):
        return r * n_col + c

    def send(x, pairs):
        return lax.ppermute(x, AXES, pairs)

    def near(phase, d):
        pairs = []
        for r in range(n_row):
            for c in range(n_col):
                x, y = divmod(c, 4)
                if (r % 2 == 0) == (phase == 1):
                    pairs.append((at(r, c), at(r, x * 4 + (y + d) % 4)))
                else:
                    pairs.append((at(r, c), at(r, (x + d) % 4 * 4 + y)))
        return pairs

    every_row, every_col = range(n_row), range(n_col)

    strip, corner, keep, give = open_strip(stored)
    other = send(give, [(at(r, c), at(1 - r, c)) for r in (0, 1) for c in every_col])
    got = send(corner, [(at(r, c), at(r, c + 4)) for r in (0, 1) for c in (0, 1)])
    corner = jnp.where(my_col < 4, corner, got)
    got = send(corner, [(at(r, c), at(1 - r, c)) for r in (0, 1) for c in (0, 1, 4, 5)])
    tall = send(strip, [(at(r, c), at(r + 6, c)) for r in (0, 1) for c in every_col])
    messages = pack(keep, other, corner, got)

    parts = [
        send(
            message,
            [(at(r, c), at(c % n_row, 2 * (2 * b + r) + c // n_row)) for r in (0, 1) for c in every_col],
        )
        for b, message in enumerate(messages)
    ]
    total = parts[0] + parts[1] + parts[2] + parts[3]
    block, corner = total[:, :WIDE], total[:, WIDE:]
    block, corner = lax.optimization_barrier((block, corner))

    near_y = [4 * x + y for x in range(4) for y in (0, 2)]
    got = send(corner, [(at(r, c), at(r + 2, c)) for r in (0, 1, 4, 5) for c in near_y])
    line = [block] + [send(block, near(1, d)) for d in SHIFTS[1:]]
    corner = jnp.where(depth % 2 == 0, corner, got)
    corner, tall = lax.optimization_barrier((corner, tall))
    tall = jnp.where(depth == 0, strip, tall)
    got_tall = send(tall, [(at(r, c), at(t, c)) for r, t in ((0, 2), (1, 3), (6, 4), (7, 5)) for c in every_col])
    got = send(corner, [(at(r, c), at(r, c + 1)) for r in every_row for c in near_y])
    corner = jnp.where(my_col % 2 == 0, corner, got)
    line = jnp.stack(line)
    corner, line = lax.optimization_barrier((corner, line))

    row_parts = [line] + [send(line, near(2, d)) for d in SHIFTS[1:]]
    swap = [(at(r, c), at(r + 1 - 2 * (r % 2), c)) for r in every_row for c in every_col]
    other = send(corner, swap)
    lower, inverse = head(corner, other)
    inverse, got_tall, tall, stored = lax.optimization_barrier((inverse, got_tall, tall, stored))

    tall = jnp.where(depth % 3 == 0, tall, got_tall)
    beside = send(tall, swap)
    held = hold(stored.reshape(-1, BLOCK, stored.shape[1]))
    return update(lower, inverse, row_parts, [tall, beside], held)


def solution(mesh):
    body = functools.partial(on_device, n_row=mesh.shape["row"], n_col=mesh.shape["col"])
    return jax.shard_map(
        body,
        mesh=mesh,
        in_specs=(P("row", "col"),),
        out_specs=(P("row", "col"), P("row", None)),
        check_vma=False,
    )
```

```python
import functools

import jax
import jax.numpy as jnp
from jax import lax
from jax.experimental import pallas as pl
from jax.experimental.pallas import tpu as pltpu
from jax.sharding import PartitionSpec as P

BLOCK = 128
WIDE = 2 * BLOCK
GROUP = 8
SHIFTS = (0, 1, 3, 2)
ORDER = (0, 1, 2, 3)
F32 = jnp.float32
BF16 = jnp.bfloat16
AXES = ("row", "col")
NT = (((1,), (1,)), ((), ()))
NN = (((1,), (0,)), ((), ()))


def exact(left, right, dims):
    return lax.dot_general(
        left, right, dims, precision=lax.Precision.HIGHEST, preferred_element_type=F32
    )


def eliminate(matrix):
    lane = lax.broadcasted_iota(jnp.int32, (8, BLOCK), 1)
    sub = lax.broadcasted_iota(jnp.int32, (8, BLOCK), 0)
    rows = [matrix[8 * i : 8 * i + 8, :] for i in range(BLOCK // 8)]
    for first in range(0, BLOCK, GROUP):
        at = first // 8
        cols = {}
        for j in range(GROUP):
            for i in range(at, BLOCK // 8):
                cols[j, i] = jnp.broadcast_to(rows[i][:, first + j : first + j + 1], (8, BLOCK))
        for j in range(GROUP):
            k = first + j
            s = k % 8
            here = lane == k
            pivot = 1.0 / cols[j, at][s : s + 1, :]
            row = jnp.where(here[:1], 1.0, rows[at][s : s + 1, :])
            heads = {m: cols[m, at][s : s + 1, :] for m in range(j + 1, GROUP)}
            for i in range(at, BLOCK // 8):
                factor = cols[j, i] * pivot
                if i == at:
                    factor = jnp.where(sub > s, factor, 0.0)
                    rows[i] = jnp.where(here & (sub > s), 0.0, rows[i]) - factor * row
                else:
                    rows[i] = jnp.where(here, 0.0, rows[i]) - factor * row
                for m in range(j + 1, GROUP):
                    cols[m, i] = cols[m, i] - factor * heads[m]
    return jnp.concatenate(rows, axis=0)


def factor_block(matrix):
    done = eliminate(matrix)
    r = lax.broadcasted_iota(jnp.int32, (BLOCK, BLOCK), 0)
    c = lax.broadcasted_iota(jnp.int32, (BLOCK, BLOCK), 1)
    pivots = jnp.sum(jnp.where(r == c, done, 0.0), axis=1, keepdims=True)
    scale = lax.rsqrt(pivots)
    scale = scale * (1.5 - 0.5 * pivots * scale * scale)
    upper = jnp.where(r <= c, done, 0.0) * scale
    inverse = jnp.where(r > c, done, jnp.where(r == c, 1.0, 0.0)) * scale
    return upper.T, inverse


def head_kernel(mine_ref, other_ref, lower_ref, inverse_ref):
    first = lax.axis_index("row") % 2 == 0
    zero = jnp.zeros((BLOCK, BLOCK), F32)
    l00, i00 = factor_block(jnp.where(first, mine_ref[:, :BLOCK], other_ref[:, :BLOCK]))
    l10 = exact(jnp.where(first, mine_ref[:, BLOCK:], other_ref[:, BLOCK:]), i00, NT)
    rest = jnp.where(first, other_ref[:, BLOCK:], mine_ref[:, BLOCK:]) - exact(l10, l10, NT)
    l11, i11 = factor_block(rest)
    i10 = -exact(i11, exact(l10, i00, NN), NN)
    lower_ref[0, :, :BLOCK] = l00
    lower_ref[0, :, BLOCK:] = zero
    lower_ref[1, :, :BLOCK] = l10
    lower_ref[1, :, BLOCK:] = l11
    inverse_ref[:BLOCK, :BLOCK] = i00
    inverse_ref[:BLOCK, BLOCK:] = zero
    inverse_ref[BLOCK:, :BLOCK] = i10
    inverse_ref[BLOCK:, BLOCK:] = i11


def head(mine, other):
    return pl.pallas_call(
        head_kernel,
        out_shape=(
            jax.ShapeDtypeStruct((2, BLOCK, WIDE), F32),
            jax.ShapeDtypeStruct((WIDE, WIDE), F32),
        ),
        cost_estimate=pl.CostEstimate(flops=10**8, bytes_accessed=10**6, transcendentals=0),
        compiler_params=pltpu.CompilerParams(vmem_limit_bytes=20 * 2**20),
        name="head",
    )(mine, other)


def hold_kernel(stored_ref, held_ref, sem):
    copy = pltpu.make_async_copy(stored_ref, held_ref, sem)
    copy.start()
    copy.wait()


def hold(stored):
    return pl.pallas_call(
        hold_kernel,
        in_specs=[pl.BlockSpec(memory_space=pltpu.HBM)],
        out_specs=pl.BlockSpec(memory_space=pltpu.VMEM),
        out_shape=pltpu.VMEM(stored.shape, F32),
        scratch_shapes=[pltpu.SemaphoreType.DMA(())],
        compiler_params=pltpu.CompilerParams(vmem_limit_bytes=46 * 2**20),
        cost_estimate=pl.CostEstimate(flops=0, bytes_accessed=2**23, transcendentals=0),
        name="hold",
    )(stored)


def open_kernel(stored_ref, strip_ref, corner_ref, keep_ref, give_ref, sem):
    copy = pltpu.make_async_copy(stored_ref.at[pl.ds(0, BLOCK)], strip_ref, sem)
    copy.start()
    first = lax.axis_index("row") % 2 == 0
    copy.wait()
    corner_ref[...] = strip_ref[:, :BLOCK]
    for b in range(keep_ref.shape[0]):
        even = strip_ref[:, 2 * b * BLOCK : (2 * b + 1) * BLOCK]
        odd = strip_ref[:, (2 * b + 1) * BLOCK : (2 * b + 2) * BLOCK]
        keep_ref[b] = jnp.where(first, even, odd).T
        give_ref[b] = jnp.where(first, odd, even).T


def open_strip(stored):
    cols = stored.shape[1]
    one = jax.ShapeDtypeStruct((BLOCK, BLOCK), F32)
    part = jax.ShapeDtypeStruct((cols // WIDE, BLOCK, BLOCK), F32)
    return pl.pallas_call(
        open_kernel,
        in_specs=[pl.BlockSpec(memory_space=pl.ANY)],
        out_shape=(jax.ShapeDtypeStruct((BLOCK, cols), F32), one, part, part),
        scratch_shapes=[pltpu.SemaphoreType.DMA(())],
        name="open",
    )(stored)


def pack_kernel(keep_ref, other_ref, corner_ref, beside_ref, *out_refs):
    first = lax.axis_index("row") % 2 == 0
    upper = jnp.where(first, corner_ref[...], beside_ref[...])
    lower = jnp.where(first, beside_ref[...], corner_ref[...])
    count = keep_ref.shape[0]
    for shift, out_ref in zip(ORDER, out_refs, strict=True):
        b = (lax.axis_index("col") // 4 + shift) % count
        out_ref[:, :BLOCK] = jnp.where(first, keep_ref[b], other_ref[b])
        out_ref[:, BLOCK:WIDE] = jnp.where(first, other_ref[b], keep_ref[b])
        out_ref[:, WIDE : WIDE + BLOCK] = upper
        out_ref[:, WIDE + BLOCK :] = lower


def pack(keep, other, corner, beside):
    return pl.pallas_call(
        pack_kernel,
        out_shape=(jax.ShapeDtypeStruct((BLOCK, 2 * WIDE), F32),) * keep.shape[0],
        name="pack",
    )(keep, other, corner, beside)


def split(x):
    high = x.astype(BF16)
    return high, (x - high.astype(F32)).astype(BF16)


def update_kernel(
    lower_ref, inverse_ref, row0_ref, row1_ref, row2_ref, row3_ref, tall_ref, beside_ref, a_ref, out_ref, factor_ref,
    a_buf, row_buf, factor_buf, col_buf, right_ref, row_sem, col_sem, out_sem, factor_sem,
):
    my_row = lax.axis_index("row")
    my_col = lax.axis_index("col")
    x, y = my_col // 4, my_col % 4
    even = my_row % 2 == 0
    count, _, cols = a_ref.shape
    blocks = cols // BLOCK

    place = []
    for far in SHIFTS:
        for near in SHIFTS:
            dx = jnp.where(even, far, near)
            dy = jnp.where(even, near, far)
            place.append((x - dx + 4) % 4 * 4 + (y - dy + 4) % 4)

    def start(src, dst, sem):
        copy = pltpu.make_async_copy(src, dst, sem)
        copy.start()
        return copy

    core = my_row % 2
    col_in = [
        start(tall_ref, col_buf.at[core], col_sem.at[0]),
        start(beside_ref, col_buf.at[1 - core], col_sem.at[1]),
    ]
    row_in = [
        start(ref, row_buf.at[a], row_sem.at[a])
        for a, ref in enumerate((row0_ref, row1_ref, row2_ref, row3_ref))
    ]

    high, low = split(inverse_ref[...])
    by_left = jnp.concatenate([high, high, low], axis=1)
    by_right = jnp.concatenate([high, low, high], axis=1)
    for copy in col_in:
        copy.wait()
    for b in range(0, blocks, 2):
        span = slice(b * BLOCK, (b + 2) * BLOCK)
        high, low = split(jnp.concatenate([col_buf[0, :, span], col_buf[1, :, span]], axis=0))
        stack = jnp.concatenate([high, low, high], axis=0)
        part = lax.dot_general(by_left, stack, NN, preferred_element_type=F32)
        if b == 0:
            known = jnp.concatenate([lower_ref[jnp.minimum(my_col, 1)].T, part[:, BLOCK:]], axis=1)
            part = jnp.where(my_col < 2, known, part)
        high, low = split(part)
        right_ref[0:WIDE, span] = high
        right_ref[WIDE : 2 * WIDE, span] = low
        right_ref[2 * WIDE : 3 * WIDE, span] = high

    out = []
    for a in range(4):
        row_in[a].wait()
        high, low = split(row_buf[a].reshape(4 * BLOCK, WIDE))
        left = jnp.concatenate([high, high, low], axis=1)
        part = lax.dot_general(left, by_right, NT, preferred_element_type=F32)
        factor_buf[a] = part.reshape(4, BLOCK, WIDE)
        for s in range(4):
            t = 4 * a + s

            @pl.when((my_row < 2) & (place[t] == 0))
            def _():
                factor_buf[a, s] = lower_ref[jnp.minimum(my_row, 1)]

        for s in range(4):
            t = 4 * a + s
            out.append(start(factor_buf.at[a, s], factor_ref.at[place[t]], factor_sem.at[t]))
        high, low = split(factor_buf[a].reshape(4 * BLOCK, WIDE))
        left = jnp.concatenate([high, high, low], axis=1)
        for n in range(0, cols, WIDE):
            span = slice(n, n + WIDE)
            part = lax.dot_general(left, right_ref[:, span], NN, preferred_element_type=F32)
            for s in range(4):
                t = 4 * a + s
                a_buf[t, :, span] = a_ref[place[t], :, span] - part[s * BLOCK : (s + 1) * BLOCK]
        for s in range(4):
            t = 4 * a + s
            out.append(start(a_buf.at[t], out_ref.at[place[t]], out_sem.at[t]))
    for copy in out:
        copy.wait()


def update(lower, inverse, row_parts, col_parts, held):
    count, _, cols = held.shape
    rows = count * BLOCK
    here = pl.BlockSpec(memory_space=pltpu.VMEM)
    there = pl.BlockSpec(memory_space=pltpu.HBM)
    trailing, factor = pl.pallas_call(
        update_kernel,
        in_specs=[here] * 2 + [there] * 6 + [here],
        out_specs=[there] * 2,
        out_shape=(
            jax.ShapeDtypeStruct((count, BLOCK, cols), F32),
            jax.ShapeDtypeStruct((count, BLOCK, WIDE), F32),
        ),
        scratch_shapes=[
            pltpu.VMEM((count, BLOCK, cols), F32),
            pltpu.VMEM((4, 4, BLOCK, WIDE), F32),
            pltpu.VMEM((4, 4, BLOCK, WIDE), F32),
            pltpu.VMEM((2, BLOCK, cols), F32),
            pltpu.VMEM((3 * WIDE, cols), BF16),
            pltpu.SemaphoreType.DMA((4,)),
            pltpu.SemaphoreType.DMA((2,)),
            pltpu.SemaphoreType.DMA((count,)),
            pltpu.SemaphoreType.DMA((count,)),
        ],
        compiler_params=pltpu.CompilerParams(vmem_limit_bytes=30 * 2**20),
        name="update",
    )(lower, inverse, *row_parts, *col_parts, held)
    return trailing.reshape(rows, cols), factor.reshape(rows, WIDE)


def on_device(stored, n_row, n_col):
    my_row = lax.axis_index("row")
    my_col = lax.axis_index("col")
    core = my_row % 2
    depth = my_row // 2

    def at(r, c):
        return r * n_col + c

    def send(x, pairs):
        return lax.ppermute(x, AXES, pairs)

    def near(phase, d):
        pairs = []
        for r in range(n_row):
            for c in range(n_col):
                x, y = divmod(c, 4)
                if (r % 2 == 0) == (phase == 1):
                    pairs.append((at(r, c), at(r, x * 4 + (y + d) % 4)))
                else:
                    pairs.append((at(r, c), at(r, (x + d) % 4 * 4 + y)))
        return pairs

    every_row, every_col = range(n_row), range(n_col)

    strip, corner, keep, give = open_strip(stored)
    other = send(give, [(at(r, c), at(1 - r, c)) for r in (0, 1) for c in every_col])
    got = send(corner, [(at(r, c), at(r, c + 4)) for r in (0, 1) for c in (0, 1)])
    corner = jnp.where(my_col < 4, corner, got)
    got = send(corner, [(at(r, c), at(1 - r, c)) for r in (0, 1) for c in (0, 1, 4, 5)])
    tall = send(strip, [(at(r, c), at(r + 6, c)) for r in (0, 1) for c in every_col])
    messages = pack(keep, other, corner, got)

    parts = [
        send(
            message,
            [
                (at(r, c), at(c % n_row, 2 * (2 * ((c // 4 + shift) % 4) + r) + c // n_row))
                for r in (0, 1)
                for c in every_col
            ],
        )
        for shift, message in zip(ORDER, messages, strict=True)
    ]
    total = parts[0] + parts[1] + parts[2] + parts[3]
    block, corner = total[:, :WIDE], total[:, WIDE:]
    block, corner = lax.optimization_barrier((block, corner))

    near_y = [4 * x + y for x in range(4) for y in (0, 2)]
    got = send(corner, [(at(r, c), at(r + 2, c)) for r in (0, 1, 4, 5) for c in near_y])
    line = [block] + [send(block, near(1, d)) for d in SHIFTS[1:]]
    corner = jnp.where(depth % 2 == 0, corner, got)
    corner, tall = lax.optimization_barrier((corner, tall))
    tall = jnp.where(depth == 0, strip, tall)
    got_tall = send(tall, [(at(r, c), at(t, c)) for r, t in ((0, 2), (1, 3), (6, 4), (7, 5)) for c in every_col])
    got = send(corner, [(at(r, c), at(r, c + 1)) for r in every_row for c in near_y])
    corner = jnp.where(my_col % 2 == 0, corner, got)
    line = jnp.stack(line)
    corner, line = lax.optimization_barrier((corner, line))

    row_parts = [line] + [send(line, near(2, d)) for d in SHIFTS[1:]]
    swap = [(at(r, c), at(r + 1 - 2 * (r % 2), c)) for r in every_row for c in every_col]
    other = send(corner, swap)
    lower, inverse = head(corner, other)
    inverse, got_tall, tall, stored = lax.optimization_barrier((inverse, got_tall, tall, stored))

    tall = jnp.where(depth % 3 == 0, tall, got_tall)
    beside = send(tall, swap)
    held = hold(stored.reshape(-1, BLOCK, stored.shape[1]))
    return update(lower, inverse, row_parts, [tall, beside], held)


def solution(mesh):
    body = functools.partial(on_device, n_row=mesh.shape["row"], n_col=mesh.shape["col"])
    return jax.shard_map(
        body,
        mesh=mesh,
        in_specs=(P("row", "col"),),
        out_specs=(P("row", "col"), P("row", None)),
        check_vma=False,
    )
```

```python
import functools

import jax
import jax.numpy as jnp
from jax import lax
from jax.experimental import pallas as pl
from jax.experimental.pallas import tpu as pltpu
from jax.sharding import PartitionSpec as P

BLOCK = 128
WIDE = 2 * BLOCK
GROUP = 8
SHIFTS = (0, 1, 3, 2)
ORDER = (0, 1, 3, 2)
F32 = jnp.float32
BF16 = jnp.bfloat16
AXES = ("row", "col")
NT = (((1,), (1,)), ((), ()))
NN = (((1,), (0,)), ((), ()))


def exact(left, right, dims):
    return lax.dot_general(
        left, right, dims, precision=lax.Precision.HIGHEST, preferred_element_type=F32
    )


def eliminate(matrix):
    lane = lax.broadcasted_iota(jnp.int32, (8, BLOCK), 1)
    sub = lax.broadcasted_iota(jnp.int32, (8, BLOCK), 0)
    rows = [matrix[8 * i : 8 * i + 8, :] for i in range(BLOCK // 8)]
    for first in range(0, BLOCK, GROUP):
        at = first // 8
        cols = {}
        for j in range(GROUP):
            for i in range(at, BLOCK // 8):
                cols[j, i] = jnp.broadcast_to(rows[i][:, first + j : first + j + 1], (8, BLOCK))
        for j in range(GROUP):
            k = first + j
            s = k % 8
            here = lane == k
            pivot = 1.0 / cols[j, at][s : s + 1, :]
            row = jnp.where(here[:1], 1.0, rows[at][s : s + 1, :])
            heads = {m: cols[m, at][s : s + 1, :] for m in range(j + 1, GROUP)}
            for i in range(at, BLOCK // 8):
                factor = cols[j, i] * pivot
                if i == at:
                    factor = jnp.where(sub > s, factor, 0.0)
                    rows[i] = jnp.where(here & (sub > s), 0.0, rows[i]) - factor * row
                else:
                    rows[i] = jnp.where(here, 0.0, rows[i]) - factor * row
                for m in range(j + 1, GROUP):
                    cols[m, i] = cols[m, i] - factor * heads[m]
    return jnp.concatenate(rows, axis=0)


def factor_block(matrix):
    done = eliminate(matrix)
    r = lax.broadcasted_iota(jnp.int32, (BLOCK, BLOCK), 0)
    c = lax.broadcasted_iota(jnp.int32, (BLOCK, BLOCK), 1)
    pivots = jnp.sum(jnp.where(r == c, done, 0.0), axis=1, keepdims=True)
    scale = lax.rsqrt(pivots)
    scale = scale * (1.5 - 0.5 * pivots * scale * scale)
    upper = jnp.where(r <= c, done, 0.0) * scale
    inverse = jnp.where(r > c, done, jnp.where(r == c, 1.0, 0.0)) * scale
    return upper.T, inverse


def head_kernel(mine_ref, other_ref, lower_ref, inverse_ref):
    first = lax.axis_index("row") % 2 == 0
    zero = jnp.zeros((BLOCK, BLOCK), F32)
    l00, i00 = factor_block(jnp.where(first, mine_ref[:, :BLOCK], other_ref[:, :BLOCK]))
    l10 = exact(jnp.where(first, mine_ref[:, BLOCK:], other_ref[:, BLOCK:]), i00, NT)
    rest = jnp.where(first, other_ref[:, BLOCK:], mine_ref[:, BLOCK:]) - exact(l10, l10, NT)
    l11, i11 = factor_block(rest)
    i10 = -exact(i11, exact(l10, i00, NN), NN)
    lower_ref[0, :, :BLOCK] = l00
    lower_ref[0, :, BLOCK:] = zero
    lower_ref[1, :, :BLOCK] = l10
    lower_ref[1, :, BLOCK:] = l11
    inverse_ref[:BLOCK, :BLOCK] = i00
    inverse_ref[:BLOCK, BLOCK:] = zero
    inverse_ref[BLOCK:, :BLOCK] = i10
    inverse_ref[BLOCK:, BLOCK:] = i11


def head(mine, other):
    return pl.pallas_call(
        head_kernel,
        out_shape=(
            jax.ShapeDtypeStruct((2, BLOCK, WIDE), F32),
            jax.ShapeDtypeStruct((WIDE, WIDE), F32),
        ),
        cost_estimate=pl.CostEstimate(flops=10**8, bytes_accessed=10**6, transcendentals=0),
        compiler_params=pltpu.CompilerParams(vmem_limit_bytes=20 * 2**20),
        name="head",
    )(mine, other)


def hold_kernel(stored_ref, held_ref, sem):
    copy = pltpu.make_async_copy(stored_ref, held_ref, sem)
    copy.start()
    copy.wait()


def hold(stored):
    return pl.pallas_call(
        hold_kernel,
        in_specs=[pl.BlockSpec(memory_space=pltpu.HBM)],
        out_specs=pl.BlockSpec(memory_space=pltpu.VMEM),
        out_shape=pltpu.VMEM(stored.shape, F32),
        scratch_shapes=[pltpu.SemaphoreType.DMA(())],
        compiler_params=pltpu.CompilerParams(vmem_limit_bytes=46 * 2**20),
        cost_estimate=pl.CostEstimate(flops=0, bytes_accessed=2**23, transcendentals=0),
        name="hold",
    )(stored)


def open_kernel(stored_ref, strip_ref, corner_ref, keep_ref, give_ref, sem):
    copy = pltpu.make_async_copy(stored_ref.at[pl.ds(0, BLOCK)], strip_ref, sem)
    copy.start()
    first = lax.axis_index("row") % 2 == 0
    copy.wait()
    corner_ref[...] = strip_ref[:, :BLOCK]
    for b in range(keep_ref.shape[0]):
        even = strip_ref[:, 2 * b * BLOCK : (2 * b + 1) * BLOCK]
        odd = strip_ref[:, (2 * b + 1) * BLOCK : (2 * b + 2) * BLOCK]
        keep_ref[b] = jnp.where(first, even, odd).T
        give_ref[b] = jnp.where(first, odd, even).T


def open_strip(stored):
    cols = stored.shape[1]
    one = jax.ShapeDtypeStruct((BLOCK, BLOCK), F32)
    part = jax.ShapeDtypeStruct((cols // WIDE, BLOCK, BLOCK), F32)
    return pl.pallas_call(
        open_kernel,
        in_specs=[pl.BlockSpec(memory_space=pl.ANY)],
        out_shape=(jax.ShapeDtypeStruct((BLOCK, cols), F32), one, part, part),
        scratch_shapes=[pltpu.SemaphoreType.DMA(())],
        name="open",
    )(stored)


def pack_kernel(keep_ref, other_ref, corner_ref, beside_ref, *out_refs):
    first = lax.axis_index("row") % 2 == 0
    upper = jnp.where(first, corner_ref[...], beside_ref[...])
    lower = jnp.where(first, beside_ref[...], corner_ref[...])
    count = keep_ref.shape[0]
    for shift, out_ref in zip(ORDER, out_refs, strict=True):
        b = (lax.axis_index("col") // 4 + shift) % count
        out_ref[:, :BLOCK] = jnp.where(first, keep_ref[b], other_ref[b])
        out_ref[:, BLOCK:WIDE] = jnp.where(first, other_ref[b], keep_ref[b])
        out_ref[:, WIDE : WIDE + BLOCK] = upper
        out_ref[:, WIDE + BLOCK :] = lower


def pack(keep, other, corner, beside):
    return pl.pallas_call(
        pack_kernel,
        out_shape=(jax.ShapeDtypeStruct((BLOCK, 2 * WIDE), F32),) * keep.shape[0],
        name="pack",
    )(keep, other, corner, beside)


def split(x):
    high = x.astype(BF16)
    return high, (x - high.astype(F32)).astype(BF16)


def update_kernel(
    lower_ref, inverse_ref, row0_ref, row1_ref, row2_ref, row3_ref, tall_ref, beside_ref, a_ref, out_ref, factor_ref,
    a_buf, row_buf, factor_buf, col_buf, right_ref, row_sem, col_sem, out_sem, factor_sem,
):
    my_row = lax.axis_index("row")
    my_col = lax.axis_index("col")
    x, y = my_col // 4, my_col % 4
    even = my_row % 2 == 0
    count, _, cols = a_ref.shape
    blocks = cols // BLOCK

    place = []
    for far in SHIFTS:
        for near in SHIFTS:
            dx = jnp.where(even, far, near)
            dy = jnp.where(even, near, far)
            place.append((x - dx + 4) % 4 * 4 + (y - dy + 4) % 4)

    def start(src, dst, sem):
        copy = pltpu.make_async_copy(src, dst, sem)
        copy.start()
        return copy

    core = my_row % 2
    col_in = [
        start(tall_ref, col_buf.at[core], col_sem.at[0]),
        start(beside_ref, col_buf.at[1 - core], col_sem.at[1]),
    ]
    row_in = [
        start(ref, row_buf.at[a], row_sem.at[a])
        for a, ref in enumerate((row0_ref, row1_ref, row2_ref, row3_ref))
    ]

    high, low = split(inverse_ref[...])
    by_left = jnp.concatenate([high, high, low], axis=1)
    by_right = jnp.concatenate([high, low, high], axis=1)
    for copy in col_in:
        copy.wait()
    for b in range(0, blocks, 2):
        span = slice(b * BLOCK, (b + 2) * BLOCK)
        high, low = split(jnp.concatenate([col_buf[0, :, span], col_buf[1, :, span]], axis=0))
        stack = jnp.concatenate([high, low, high], axis=0)
        part = lax.dot_general(by_left, stack, NN, preferred_element_type=F32)
        if b == 0:
            known = jnp.concatenate([lower_ref[jnp.minimum(my_col, 1)].T, part[:, BLOCK:]], axis=1)
            part = jnp.where(my_col < 2, known, part)
        high, low = split(part)
        right_ref[0:WIDE, span] = high
        right_ref[WIDE : 2 * WIDE, span] = low
        right_ref[2 * WIDE : 3 * WIDE, span] = high

    out = []
    for a in range(4):
        row_in[a].wait()
        high, low = split(row_buf[a].reshape(4 * BLOCK, WIDE))
        left = jnp.concatenate([high, high, low], axis=1)
        part = lax.dot_general(left, by_right, NT, preferred_element_type=F32)
        factor_buf[a] = part.reshape(4, BLOCK, WIDE)
        for s in range(4):
            t = 4 * a + s

            @pl.when((my_row < 2) & (place[t] == 0))
            def _():
                factor_buf[a, s] = lower_ref[jnp.minimum(my_row, 1)]

        for s in range(4):
            t = 4 * a + s
            out.append(start(factor_buf.at[a, s], factor_ref.at[place[t]], factor_sem.at[t]))
        high, low = split(factor_buf[a].reshape(4 * BLOCK, WIDE))
        left = jnp.concatenate([high, high, low], axis=1)
        for n in range(0, cols, 2 * WIDE):
            span = slice(n, n + 2 * WIDE)
            part = lax.dot_general(left, right_ref[:, span], NN, preferred_element_type=F32)
            for s in range(4):
                t = 4 * a + s
                a_buf[t, :, span] = a_ref[place[t], :, span] - part[s * BLOCK : (s + 1) * BLOCK]
        for s in range(4):
            t = 4 * a + s
            out.append(start(a_buf.at[t], out_ref.at[place[t]], out_sem.at[t]))
    for copy in out:
        copy.wait()


def update(lower, inverse, row_parts, col_parts, held):
    count, _, cols = held.shape
    rows = count * BLOCK
    here = pl.BlockSpec(memory_space=pltpu.VMEM)
    there = pl.BlockSpec(memory_space=pltpu.HBM)
    trailing, factor = pl.pallas_call(
        update_kernel,
        in_specs=[here] * 2 + [there] * 6 + [here],
        out_specs=[there] * 2,
        out_shape=(
            jax.ShapeDtypeStruct((count, BLOCK, cols), F32),
            jax.ShapeDtypeStruct((count, BLOCK, WIDE), F32),
        ),
        scratch_shapes=[
            pltpu.VMEM((count, BLOCK, cols), F32),
            pltpu.VMEM((4, 4, BLOCK, WIDE), F32),
            pltpu.VMEM((4, 4, BLOCK, WIDE), F32),
            pltpu.VMEM((2, BLOCK, cols), F32),
            pltpu.VMEM((3 * WIDE, cols), BF16),
            pltpu.SemaphoreType.DMA((4,)),
            pltpu.SemaphoreType.DMA((2,)),
            pltpu.SemaphoreType.DMA((count,)),
            pltpu.SemaphoreType.DMA((count,)),
        ],
        compiler_params=pltpu.CompilerParams(vmem_limit_bytes=30 * 2**20),
        name="update",
    )(lower, inverse, *row_parts, *col_parts, held)
    return trailing.reshape(rows, cols), factor.reshape(rows, WIDE)


def on_device(stored, n_row, n_col):
    my_row = lax.axis_index("row")
    my_col = lax.axis_index("col")
    core = my_row % 2
    depth = my_row // 2

    def at(r, c):
        return r * n_col + c

    def send(x, pairs):
        return lax.ppermute(x, AXES, pairs)

    def near(phase, d):
        pairs = []
        for r in range(n_row):
            for c in range(n_col):
                x, y = divmod(c, 4)
                if (r % 2 == 0) == (phase == 1):
                    pairs.append((at(r, c), at(r, x * 4 + (y + d) % 4)))
                else:
                    pairs.append((at(r, c), at(r, (x + d) % 4 * 4 + y)))
        return pairs

    every_row, every_col = range(n_row), range(n_col)

    strip, corner, keep, give = open_strip(stored)
    other = send(give, [(at(r, c), at(1 - r, c)) for r in (0, 1) for c in every_col])
    got = send(corner, [(at(r, c), at(r, c + 4)) for r in (0, 1) for c in (0, 1)])
    corner = jnp.where(my_col < 4, corner, got)
    got = send(corner, [(at(r, c), at(1 - r, c)) for r in (0, 1) for c in (0, 1, 4, 5)])
    tall = send(strip, [(at(r, c), at(r + 6, c)) for r in (0, 1) for c in every_col])
    messages = pack(keep, other, corner, got)

    parts = [
        send(
            message,
            [
                (at(r, c), at(c % n_row, 2 * (2 * ((c // 4 + shift) % 4) + r) + c // n_row))
                for r in (0, 1)
                for c in every_col
            ],
        )
        for shift, message in zip(ORDER, messages, strict=True)
    ]
    total = parts[0] + parts[1] + parts[2] + parts[3]
    block, corner = total[:, :WIDE], total[:, WIDE:]
    block, corner = lax.optimization_barrier((block, corner))

    near_y = [4 * x + y for x in range(4) for y in (0, 2)]
    got = send(corner, [(at(r, c), at(r + 2, c)) for r in (0, 1, 4, 5) for c in near_y])
    line = [block] + [send(block, near(1, d)) for d in SHIFTS[1:]]
    corner = jnp.where(depth % 2 == 0, corner, got)
    corner, tall = lax.optimization_barrier((corner, tall))
    tall = jnp.where(depth == 0, strip, tall)
    got_tall = send(tall, [(at(r, c), at(t, c)) for r, t in ((0, 2), (1, 3), (6, 4), (7, 5)) for c in every_col])
    got = send(corner, [(at(r, c), at(r, c + 1)) for r in every_row for c in near_y])
    corner = jnp.where(my_col % 2 == 0, corner, got)
    line = jnp.stack(line)
    corner, line = lax.optimization_barrier((corner, line))

    row_parts = [line] + [send(line, near(2, d)) for d in SHIFTS[1:]]
    swap = [(at(r, c), at(r + 1 - 2 * (r % 2), c)) for r in every_row for c in every_col]
    other = send(corner, swap)
    lower, inverse = head(corner, other)
    inverse, got_tall, tall, stored = lax.optimization_barrier((inverse, got_tall, tall, stored))

    tall = jnp.where(depth % 3 == 0, tall, got_tall)
    beside = send(tall, swap)
    held = hold(stored.reshape(-1, BLOCK, stored.shape[1]))
    return update(lower, inverse, row_parts, [tall, beside], held)


def solution(mesh):
    body = functools.partial(on_device, n_row=mesh.shape["row"], n_col=mesh.shape["col"])
    return jax.shard_map(
        body,
        mesh=mesh,
        in_specs=(P("row", "col"),),
        out_specs=(P("row", "col"), P("row", None)),
        check_vma=False,
    )
```

```python
import functools

import jax
import jax.numpy as jnp
from jax import lax
from jax.experimental import pallas as pl
from jax.experimental.pallas import tpu as pltpu
from jax.sharding import PartitionSpec as P

BLOCK = 128
WIDE = 2 * BLOCK
GROUP = 8
SHIFTS = (0, 1, 3, 2)
ORDER = (0, 1, 3, 2)
F32 = jnp.float32
BF16 = jnp.bfloat16
AXES = ("row", "col")
NT = (((1,), (1,)), ((), ()))
NN = (((1,), (0,)), ((), ()))


def exact(left, right, dims):
    return lax.dot_general(
        left, right, dims, precision=lax.Precision.HIGHEST, preferred_element_type=F32
    )


def eliminate(matrix):
    lane = lax.broadcasted_iota(jnp.int32, (8, BLOCK), 1)
    sub = lax.broadcasted_iota(jnp.int32, (8, BLOCK), 0)
    rows = [matrix[8 * i : 8 * i + 8, :] for i in range(BLOCK // 8)]
    for first in range(0, BLOCK, GROUP):
        at = first // 8
        cols = {}
        for j in range(GROUP):
            for i in range(at, BLOCK // 8):
                cols[j, i] = jnp.broadcast_to(rows[i][:, first + j : first + j + 1], (8, BLOCK))
        for j in range(GROUP):
            k = first + j
            s = k % 8
            here = lane == k
            pivot = 1.0 / cols[j, at][s : s + 1, :]
            row = jnp.where(here[:1], 1.0, rows[at][s : s + 1, :])
            heads = {m: cols[m, at][s : s + 1, :] for m in range(j + 1, GROUP)}
            for i in range(at, BLOCK // 8):
                factor = cols[j, i] * pivot
                if i == at:
                    factor = jnp.where(sub > s, factor, 0.0)
                    rows[i] = jnp.where(here & (sub > s), 0.0, rows[i]) - factor * row
                else:
                    rows[i] = jnp.where(here, 0.0, rows[i]) - factor * row
                for m in range(j + 1, GROUP):
                    cols[m, i] = cols[m, i] - factor * heads[m]
    return jnp.concatenate(rows, axis=0)


def factor_block(matrix):
    done = eliminate(matrix)
    r = lax.broadcasted_iota(jnp.int32, (BLOCK, BLOCK), 0)
    c = lax.broadcasted_iota(jnp.int32, (BLOCK, BLOCK), 1)
    pivots = jnp.sum(jnp.where(r == c, done, 0.0), axis=1, keepdims=True)
    scale = lax.rsqrt(pivots)
    scale = scale * (1.5 - 0.5 * pivots * scale * scale)
    upper = jnp.where(r <= c, done, 0.0) * scale
    inverse = jnp.where(r > c, done, jnp.where(r == c, 1.0, 0.0)) * scale
    return upper.T, inverse


def head_kernel(mine_ref, other_ref, lower_ref, inverse_ref):
    first = lax.axis_index("row") % 2 == 0
    zero = jnp.zeros((BLOCK, BLOCK), F32)
    l00, i00 = factor_block(jnp.where(first, mine_ref[:, :BLOCK], other_ref[:, :BLOCK]))
    l10 = exact(jnp.where(first, mine_ref[:, BLOCK:], other_ref[:, BLOCK:]), i00, NT)
    rest = jnp.where(first, other_ref[:, BLOCK:], mine_ref[:, BLOCK:]) - exact(l10, l10, NT)
    l11, i11 = factor_block(rest)
    i10 = -exact(i11, exact(l10, i00, NN), NN)
    lower_ref[0, :, :BLOCK] = l00
    lower_ref[0, :, BLOCK:] = zero
    lower_ref[1, :, :BLOCK] = l10
    lower_ref[1, :, BLOCK:] = l11
    inverse_ref[:BLOCK, :BLOCK] = i00
    inverse_ref[:BLOCK, BLOCK:] = zero
    inverse_ref[BLOCK:, :BLOCK] = i10
    inverse_ref[BLOCK:, BLOCK:] = i11


def head(mine, other):
    return pl.pallas_call(
        head_kernel,
        out_shape=(
            jax.ShapeDtypeStruct((2, BLOCK, WIDE), F32),
            jax.ShapeDtypeStruct((WIDE, WIDE), F32),
        ),
        cost_estimate=pl.CostEstimate(flops=10**8, bytes_accessed=10**6, transcendentals=0),
        compiler_params=pltpu.CompilerParams(vmem_limit_bytes=20 * 2**20),
        name="head",
    )(mine, other)


def hold_kernel(stored_ref, held_ref, sem):
    copy = pltpu.make_async_copy(stored_ref, held_ref, sem)
    copy.start()
    copy.wait()


def hold(stored):
    return pl.pallas_call(
        hold_kernel,
        in_specs=[pl.BlockSpec(memory_space=pltpu.HBM)],
        out_specs=pl.BlockSpec(memory_space=pltpu.VMEM),
        out_shape=pltpu.VMEM(stored.shape, F32),
        scratch_shapes=[pltpu.SemaphoreType.DMA(())],
        compiler_params=pltpu.CompilerParams(vmem_limit_bytes=46 * 2**20),
        cost_estimate=pl.CostEstimate(flops=0, bytes_accessed=2**23, transcendentals=0),
        name="hold",
    )(stored)


def open_kernel(stored_ref, strip_ref, corner_ref, keep_ref, give_ref, sem):
    copy = pltpu.make_async_copy(stored_ref.at[pl.ds(0, BLOCK)], strip_ref, sem)
    copy.start()
    first = lax.axis_index("row") % 2 == 0
    copy.wait()
    corner_ref[...] = strip_ref[:, :BLOCK]
    for b in range(keep_ref.shape[0]):
        even = strip_ref[:, 2 * b * BLOCK : (2 * b + 1) * BLOCK]
        odd = strip_ref[:, (2 * b + 1) * BLOCK : (2 * b + 2) * BLOCK]
        keep_ref[b] = jnp.where(first, even, odd).T
        give_ref[b] = jnp.where(first, odd, even).T


def open_strip(stored):
    cols = stored.shape[1]
    one = jax.ShapeDtypeStruct((BLOCK, BLOCK), F32)
    part = jax.ShapeDtypeStruct((cols // WIDE, BLOCK, BLOCK), F32)
    return pl.pallas_call(
        open_kernel,
        in_specs=[pl.BlockSpec(memory_space=pl.ANY)],
        out_shape=(jax.ShapeDtypeStruct((BLOCK, cols), F32), one, part, part),
        scratch_shapes=[pltpu.SemaphoreType.DMA(())],
        name="open",
    )(stored)


def pack_kernel(keep_ref, other_ref, corner_ref, beside_ref, *out_refs):
    first = lax.axis_index("row") % 2 == 0
    upper = jnp.where(first, corner_ref[...], beside_ref[...])
    lower = jnp.where(first, beside_ref[...], corner_ref[...])
    count = keep_ref.shape[0]
    for shift, out_ref in zip(ORDER, out_refs, strict=True):
        b = (lax.axis_index("col") // 4 + shift) % count
        out_ref[:, :BLOCK] = jnp.where(first, keep_ref[b], other_ref[b])
        out_ref[:, BLOCK:WIDE] = jnp.where(first, other_ref[b], keep_ref[b])
        out_ref[:, WIDE : WIDE + BLOCK] = upper
        out_ref[:, WIDE + BLOCK :] = lower


def pack(keep, other, corner, beside):
    return pl.pallas_call(
        pack_kernel,
        out_shape=(jax.ShapeDtypeStruct((BLOCK, 2 * WIDE), F32),) * keep.shape[0],
        name="pack",
    )(keep, other, corner, beside)


def split(x):
    high = x.astype(BF16)
    return high, (x - high.astype(F32)).astype(BF16)


def update_kernel(
    lower_ref, inverse_ref, row0_ref, row1_ref, row2_ref, row3_ref, tall_ref, beside_ref, a_ref, out_ref, factor_ref,
    a_buf, row_buf, factor_buf, col_buf, right_ref, row_sem, col_sem, out_sem, factor_sem,
):
    my_row = lax.axis_index("row")
    my_col = lax.axis_index("col")
    x, y = my_col // 4, my_col % 4
    even = my_row % 2 == 0
    count, _, cols = a_ref.shape
    blocks = cols // BLOCK

    place = []
    for far in SHIFTS:
        for near in SHIFTS:
            dx = jnp.where(even, far, near)
            dy = jnp.where(even, near, far)
            place.append((x - dx + 4) % 4 * 4 + (y - dy + 4) % 4)

    def start(src, dst, sem):
        copy = pltpu.make_async_copy(src, dst, sem)
        copy.start()
        return copy

    core = my_row % 2
    col_in = [
        start(tall_ref, col_buf.at[core], col_sem.at[0]),
        start(beside_ref, col_buf.at[1 - core], col_sem.at[1]),
    ]
    row_in = [
        start(ref, row_buf.at[a], row_sem.at[a])
        for a, ref in enumerate((row0_ref, row1_ref, row2_ref, row3_ref))
    ]

    high, low = split(inverse_ref[...])
    by_left = jnp.concatenate([high, high, low], axis=1)
    by_right = jnp.concatenate([high, low, high], axis=1)
    for copy in col_in:
        copy.wait()
    for b in range(0, blocks, 2):
        span = slice(b * BLOCK, (b + 2) * BLOCK)
        high, low = split(jnp.concatenate([col_buf[0, :, span], col_buf[1, :, span]], axis=0))
        stack = jnp.concatenate([high, low, high], axis=0)
        part = lax.dot_general(by_left, stack, NN, preferred_element_type=F32)
        if b == 0:
            known = jnp.concatenate([lower_ref[jnp.minimum(my_col, 1)].T, part[:, BLOCK:]], axis=1)
            part = jnp.where(my_col < 2, known, part)
        high, low = split(part)
        right_ref[0:WIDE, span] = high
        right_ref[WIDE : 2 * WIDE, span] = low
        right_ref[2 * WIDE : 3 * WIDE, span] = high

    out = []
    for a in range(4):
        row_in[a].wait()
        high, low = split(row_buf[a].reshape(4 * BLOCK, WIDE))
        left = jnp.concatenate([high, high, low], axis=1)
        part = lax.dot_general(left, by_right, NT, preferred_element_type=F32)
        factor_buf[a] = part.reshape(4, BLOCK, WIDE)
        for s in range(4):
            t = 4 * a + s

            @pl.when((my_row < 2) & (place[t] == 0))
            def _():
                factor_buf[a, s] = lower_ref[jnp.minimum(my_row, 1)]

        for s in range(4):
            t = 4 * a + s
            out.append(start(factor_buf.at[a, s], factor_ref.at[place[t]], factor_sem.at[t]))
        high, low = split(factor_buf[a].reshape(4 * BLOCK, WIDE))
        left = jnp.concatenate([high, high, low], axis=1)
        for n in range(0, cols, 4 * WIDE):
            span = slice(n, n + 4 * WIDE)
            part = lax.dot_general(left, right_ref[:, span], NN, preferred_element_type=F32)
            for s in range(4):
                t = 4 * a + s
                a_buf[t, :, span] = a_ref[place[t], :, span] - part[s * BLOCK : (s + 1) * BLOCK]
        for s in range(4):
            t = 4 * a + s
            out.append(start(a_buf.at[t], out_ref.at[place[t]], out_sem.at[t]))
    for copy in out:
        copy.wait()


def update(lower, inverse, row_parts, col_parts, held):
    count, _, cols = held.shape
    rows = count * BLOCK
    here = pl.BlockSpec(memory_space=pltpu.VMEM)
    there = pl.BlockSpec(memory_space=pltpu.HBM)
    trailing, factor = pl.pallas_call(
        update_kernel,
        in_specs=[here] * 2 + [there] * 6 + [here],
        out_specs=[there] * 2,
        out_shape=(
            jax.ShapeDtypeStruct((count, BLOCK, cols), F32),
            jax.ShapeDtypeStruct((count, BLOCK, WIDE), F32),
        ),
        scratch_shapes=[
            pltpu.VMEM((count, BLOCK, cols), F32),
            pltpu.VMEM((4, 4, BLOCK, WIDE), F32),
            pltpu.VMEM((4, 4, BLOCK, WIDE), F32),
            pltpu.VMEM((2, BLOCK, cols), F32),
            pltpu.VMEM((3 * WIDE, cols), BF16),
            pltpu.SemaphoreType.DMA((4,)),
            pltpu.SemaphoreType.DMA((2,)),
            pltpu.SemaphoreType.DMA((count,)),
            pltpu.SemaphoreType.DMA((count,)),
        ],
        compiler_params=pltpu.CompilerParams(vmem_limit_bytes=30 * 2**20),
        name="update",
    )(lower, inverse, *row_parts, *col_parts, held)
    return trailing.reshape(rows, cols), factor.reshape(rows, WIDE)


def on_device(stored, n_row, n_col):
    my_row = lax.axis_index("row")
    my_col = lax.axis_index("col")
    core = my_row % 2
    depth = my_row // 2

    def at(r, c):
        return r * n_col + c

    def send(x, pairs):
        return lax.ppermute(x, AXES, pairs)

    def near(phase, d):
        pairs = []
        for r in range(n_row):
            for c in range(n_col):
                x, y = divmod(c, 4)
                if (r % 2 == 0) == (phase == 1):
                    pairs.append((at(r, c), at(r, x * 4 + (y + d) % 4)))
                else:
                    pairs.append((at(r, c), at(r, (x + d) % 4 * 4 + y)))
        return pairs

    every_row, every_col = range(n_row), range(n_col)

    strip, corner, keep, give = open_strip(stored)
    other = send(give, [(at(r, c), at(1 - r, c)) for r in (0, 1) for c in every_col])
    got = send(corner, [(at(r, c), at(r, c + 4)) for r in (0, 1) for c in (0, 1)])
    corner = jnp.where(my_col < 4, corner, got)
    got = send(corner, [(at(r, c), at(1 - r, c)) for r in (0, 1) for c in (0, 1, 4, 5)])
    tall = send(strip, [(at(r, c), at(r + 6, c)) for r in (0, 1) for c in every_col])
    messages = pack(keep, other, corner, got)

    parts = [
        send(
            message,
            [
                (at(r, c), at(c % n_row, 2 * (2 * ((c // 4 + shift) % 4) + r) + c // n_row))
                for r in (0, 1)
                for c in every_col
            ],
        )
        for shift, message in zip(ORDER, messages, strict=True)
    ]
    total = parts[0] + parts[1] + parts[2] + parts[3]
    block, corner = total[:, :WIDE], total[:, WIDE:]
    block, corner = lax.optimization_barrier((block, corner))

    near_y = [4 * x + y for x in range(4) for y in (0, 2)]
    got = send(corner, [(at(r, c), at(r + 2, c)) for r in (0, 1, 4, 5) for c in near_y])
    line = [block] + [send(block, near(1, d)) for d in SHIFTS[1:]]
    corner = jnp.where(depth % 2 == 0, corner, got)
    corner, tall = lax.optimization_barrier((corner, tall))
    tall = jnp.where(depth == 0, strip, tall)
    got_tall = send(tall, [(at(r, c), at(t, c)) for r, t in ((0, 2), (1, 3), (6, 4), (7, 5)) for c in every_col])
    got = send(corner, [(at(r, c), at(r, c + 1)) for r in every_row for c in near_y])
    corner = jnp.where(my_col % 2 == 0, corner, got)
    line = jnp.stack(line)
    corner, line = lax.optimization_barrier((corner, line))

    row_parts = [line] + [send(line, near(2, d)) for d in SHIFTS[1:]]
    swap = [(at(r, c), at(r + 1 - 2 * (r % 2), c)) for r in every_row for c in every_col]
    other = send(corner, swap)
    lower, inverse = head(corner, other)
    inverse, got_tall, tall, stored = lax.optimization_barrier((inverse, got_tall, tall, stored))

    tall = jnp.where(depth % 3 == 0, tall, got_tall)
    beside = send(tall, swap)
    held = hold(stored.reshape(-1, BLOCK, stored.shape[1]))
    return update(lower, inverse, row_parts, [tall, beside], held)


def solution(mesh):
    body = functools.partial(on_device, n_row=mesh.shape["row"], n_col=mesh.shape["col"])
    return jax.shard_map(
        body,
        mesh=mesh,
        in_specs=(P("row", "col"),),
        out_specs=(P("row", "col"), P("row", None)),
        check_vma=False,
    )
```
